32 devices in a mesh: gx: 16 (over z, x, core), gy: 2 (over y).
Axes of the slice: x: 2, y: 2, z: 4, core: 2. Of those that a mesh axis runs over, the one named last changes fastest.
Arguments:
- density: float32 [128, 16, 256], P('gx', 'gy'), may hold values from 0.05 to 1
- passive: int32 [128, 16, 256], P('gx', 'gy'), may hold values 0 or 1
- fixed_nodes: int32 [128, 16, 256], P('gx', 'gy'), may hold values 0 or 1
- load_nodes: int32 [128, 16, 256], P('gx', 'gy'), may hold values 0 or 1
- port_load: float32 [3, 128, 16, 256], P(None, 'gx', 'gy'), may hold values from -12 to 12
- adjoint_guess: float32 [3, 128, 16, 256], P(None, 'gx', 'gy'), may hold values from -6 to 6
- primal: float32 [3, 128, 16, 256], P(None, 'gx', 'gy'), may hold values from -6 to 6
Outputs:
- sensitivity: float32 [128, 16, 256], P('gx', 'gy')
- adjoint: float32 [3, 128, 16, 256], P(None, 'gx', 'gy')
The draws below stay inside these ranges and needn't reach their ends.
All inputs are finite; a program needn't handle non-finite values. No bound on the sum of `passive` or of `fixed_nodes` or of `load_nodes` on one device may be relied on, other than what follows from the above.
Results may differ from the reference program's by a relative error of at most 0.00013.
Values sent between devices are 32-bit elements; how exact they have to be, the bound alone decides.
A program may use at most 64 MiB of HBM per device.

```python
import math
import jax
import jax.numpy as jnp
import numpy as np
from jax import lax

ITERS = 2
NX = 128
NY = 16
NZ = 256


def draw_port_load(key, part):
    ramp = 1.0 + 2.0 * jnp.arange(NX, dtype=jnp.float32) / (NX - 1)
    base = jnp.clip(jax.random.normal(key, (3, NX, NY, NZ), jnp.float32), -4.0, 4.0)
    return (base * ramp[None, :, None, None]).astype(jnp.float32)


def with_ends(values, stream_key, least, top_value):
    index_at = [jax.random.randint(jax.random.fold_in(stream_key, axis), (), 0, length) for axis, length in enumerate(values.shape)]
    widest = values.shape.index(max(values.shape))
    next_to = index_at[:widest] + [(index_at[widest] + 1) % values.shape[widest]] + index_at[widest + 1:]
    return values.at[tuple(index_at)].set(least).at[tuple(next_to)].set(top_value)


def shard_levels(key, dims, pieces, low, largest):
    gain = 1.0
    for axis_at, blocks in pieces:
        steps = jax.random.uniform(jax.random.fold_in(jax.random.fold_in(key, 6), axis_at), (blocks,), jnp.float32, low / len(pieces), largest / len(pieces))
        gain = gain * jnp.repeat(jnp.exp(steps), dims[axis_at] // blocks).reshape((-1,) + (1,) * (len(dims) - 1 - axis_at))
    return gain


def noise(key, shape, width, reach, cuts=(), held_as=jnp.bfloat16):
    values = jax.random.normal(key, shape, jnp.float32) * width
    if len(cuts) > 0:
        values = shard_levels(key, shape, cuts, -0.22, 0.18) * values
    return jnp.clip(values, min=-reach, max=reach).astype(held_as)


def setup_inputs(seed: int = 0) -> dict:
    keys = jax.random.split(jax.random.key(seed), 8)
    return {
        "density": jnp.clip(0.05 + 0.95 * jax.random.uniform(keys[0], (NX, NY, NZ), jnp.float32) ** shard_levels(keys[0], (NX, NY, NZ), ((0, 16), (1, 2)), -0.2, 0.2), 0.05, 1.0),
        "passive": with_ends((jax.random.randint(keys[1], (NX, NY, NZ), 0, 8) < 1).astype(jnp.int32), jax.random.fold_in(keys[1], 1), 0, 1),
        "fixed_nodes": with_ends((jax.random.randint(keys[2], (NX, NY, NZ), 0, 8) < 1).astype(jnp.int32), jax.random.fold_in(keys[2], 1), 0, 1),
        "load_nodes": with_ends((jax.random.randint(keys[3], (NX, NY, NZ), 0, 2) < 1).astype(jnp.int32), jax.random.fold_in(keys[3], 1), 0, 1),
        "port_load": draw_port_load(jax.random.fold_in(keys[7], 71), 0),
        "adjoint_guess": noise(keys[5], (3, NX, NY, NZ), 1.0, 6.0, ((1, 16), (2, 2)), jnp.float32),
        "primal": noise(keys[6], (3, NX, NY, NZ), 1.0, 6.0, ((1, 16), (2, 2)), jnp.float32),
    }


EMIN = 0.01
BETA = 4.0
ETA = 0.5
RMIN = 3.0
HIGH = lax.Precision.HIGHEST

def corner_list():
    return [(along_x, along_y, along_z) for along_x in (0, 1) for along_y in (0, 1) for along_z in (0, 1)]

def element_matrix():
    poisson = 0.3
    lame = poisson / ((1 + poisson) * (1 - 2 * poisson))
    shear = 0.5 / (1 + poisson)
    elastic = np.zeros((6, 6))
    elastic[:3, :3] = lame
    for index in range(3):
        elastic[index, index] += 2 * shear
        elastic[index + 3, index + 3] = shear
    points = [0.5 - 0.5 / math.sqrt(3.0), 0.5 + 0.5 / math.sqrt(3.0)]
    result = np.zeros((24, 24))
    for point_s in points:
        for point_t in points:
            for point_r in points:
                strain = np.zeros((6, 24))
                for index, corner in enumerate(corner_list()):
                    factor_x = point_s if corner[0] else 1 - point_s
                    factor_y = point_t if corner[1] else 1 - point_t
                    factor_z = point_r if corner[2] else 1 - point_r
                    slope_x = (2 * corner[0] - 1) * factor_y * factor_z
                    slope_y = factor_x * (2 * corner[1] - 1) * factor_z
                    slope_z = factor_x * factor_y * (2 * corner[2] - 1)
                    column = 3 * index
                    strain[0, column] = slope_x
                    strain[1, column + 1] = slope_y
                    strain[2, column + 2] = slope_z
                    strain[3, column] = slope_y
                    strain[3, column + 1] = slope_x
                    strain[4, column + 1] = slope_z
                    strain[4, column + 2] = slope_y
                    strain[5, column] = slope_z
                    strain[5, column + 2] = slope_x
                result += 0.125 * strain.T @ elastic @ strain
    return result.astype(np.float32)

def diagonal_of(matrix):
    return np.array([matrix[index, index] for index in range(24)], dtype=np.float32)

def filter_offsets():
    found = []
    for shift_x in range(-2, 3):
        for shift_y in range(-2, 3):
            for shift_z in range(-2, 3):
                square = shift_x * shift_x + shift_y * shift_y + shift_z * shift_z
                if square < 9:
                    found.append((shift_x, shift_y, shift_z, RMIN - math.sqrt(square)))
    return found

def zshift(field, amount):
    if amount == 0:
        return field
    if amount > 0:
        zeros = jnp.zeros(field.shape[:-1] + (amount,), field.dtype)
        return jnp.concatenate([field[..., amount:], zeros], axis=-1)
    zeros = jnp.zeros(field.shape[:-1] + (-amount,), field.dtype)
    return jnp.concatenate([zeros, field[..., :amount]], axis=-1)

def filter_sum(padded, start, count_x, count_y):
    total = None
    for shift_x, shift_y, shift_z, weight in filter_offsets():
        piece = padded[start + shift_x:start + shift_x + count_x, start + shift_y:start + shift_y + count_y]
        term = weight * zshift(piece, shift_z)
        total = term if total is None else total + term
    return total

def project(filtered):
    denom = 2.0 * math.tanh(BETA * ETA)
    bent = jnp.tanh(BETA * (filtered - ETA))
    return ((math.tanh(BETA * ETA) + bent) / denom, BETA * (1.0 - bent * bent) / denom)

def corner_field(padded, corner, count_x, count_y, low):
    piece = padded[:, low + corner[0]:low + corner[0] + count_x, low + corner[1]:low + corner[1] + count_y]
    return zshift(piece, corner[2])

def corner_forces(padded, table, index, count_x, count_y, low):
    total = None
    for other, corner in enumerate(corner_list()):
        block = table[3 * index:3 * index + 3, 3 * other:3 * other + 3]
        term = jnp.einsum('ij,jxyz->ixyz', block, corner_field(padded, corner, count_x, count_y, low), precision=HIGH)
        total = term if total is None else total + term
    return total

def apply_operator(padded, stiff_ext, table, count_x, count_y):
    total = None
    for index, corner in enumerate(corner_list()):
        forces = corner_forces(padded, table, index, count_x + 1, count_y + 1, 0) * stiff_ext[None]
        piece = forces[:, 1 - corner[0]:1 - corner[0] + count_x, 1 - corner[1]:1 - corner[1] + count_y]
        term = zshift(piece, -corner[2])
        total = term if total is None else total + term
    return total

def reference(density, passive, fixed_nodes, load_nodes, port_load, adjoint_guess, primal):
    count_x, count_y, count_z = density.shape
    table = jnp.asarray(element_matrix())
    diagonal_table = diagonal_of(element_matrix())
    free = (1 - fixed_nodes).astype(jnp.float32)
    solid = passive.astype(jnp.float32)
    blended = jnp.where(passive == 1, jnp.float32(1.0), density)
    wide = ((2, 2), (2, 2), (0, 0))
    weight_total = filter_sum(jnp.pad(jnp.ones_like(density), wide), 2, count_x, count_y)
    filtered = filter_sum(jnp.pad(blended, wide), 2, count_x, count_y) / weight_total
    heaviside, slope = project(filtered)
    physical = jnp.where(passive == 1, jnp.float32(1.0), heaviside)
    stiffness = EMIN + (1.0 - EMIN) * physical ** 3
    stiff_ext = jnp.pad(stiffness, ((1, 1), (1, 1), (0, 0)))[:count_x + 1, :count_y + 1]
    node_pad = ((0, 0), (1, 1), (1, 1), (0, 0))
    diagonal = None
    for index, corner in enumerate(corner_list()):
        values = jnp.asarray(diagonal_table[3 * index:3 * index + 3])
        piece = values[:, None, None, None] * stiff_ext[None]
        piece = piece[:, 1 - corner[0]:1 - corner[0] + count_x, 1 - corner[1]:1 - corner[1] + count_y]
        term = zshift(piece, -corner[2])
        diagonal = term if diagonal is None else diagonal + term
    inverse = free / diagonal

    def operator(field):
        return free * apply_operator(jnp.pad(field, node_pad), stiff_ext, table, count_x, count_y)
    load_field = (free * load_nodes.astype(jnp.float32))[None] * port_load
    solution = free[None] * adjoint_guess
    residual = load_field - operator(solution)
    precond = inverse * residual
    direction = precond
    current = jnp.sum(residual * precond)
    for step in range(ITERS):
        image = operator(direction)
        alpha = current / jnp.sum(direction * image)
        solution = solution + alpha * direction
        if step + 1 < ITERS:
            residual = residual - alpha * image
            precond = inverse * residual
            following = jnp.sum(residual * precond)
            direction = precond + following / current * direction
            current = following
    adjoint_pad = jnp.pad(solution, node_pad)
    primal_pad = jnp.pad(free[None] * primal, node_pad)
    energy = None
    for index, corner in enumerate(corner_list()):
        forces = corner_forces(primal_pad, table, index, count_x, count_y, 1)
        term = lax.optimization_barrier(jnp.sum(corner_field(adjoint_pad, corner, count_x, count_y, 1) * forces, axis=0))
        energy = term if energy is None else energy + term
    grad = -3.0 * (1.0 - EMIN) * physical ** 2 * energy * slope * (1.0 - solid)
    spread = grad / weight_total
    sensitivity = (1.0 - solid) * filter_sum(jnp.pad(spread, wide), 2, count_x, count_y)
    return (sensitivity, solution)
```

```python
import math

import jax
import jax.numpy as jnp
import numpy as np
from jax import lax
from jax.experimental import pallas as pl
from jax.experimental.pallas import tpu as pltpu
from jax.sharding import PartitionSpec as P

EMIN = 0.01
BETA = 4.0
ETA = 0.5
RMIN = 3.0
N = 8
W = 4
L = N + 2 * W
NZ = 256
MESH = pl.DeviceIdType.MESH


def corner_list():
    return [
        (along_x, along_y, along_z)
        for along_x in (0, 1)
        for along_y in (0, 1)
        for along_z in (0, 1)
    ]


def element_matrix():
    poisson = 0.3
    lame = poisson / ((1 + poisson) * (1 - 2 * poisson))
    shear = 0.5 / (1 + poisson)
    elastic = np.zeros((6, 6))
    elastic[:3, :3] = lame
    for index in range(3):
        elastic[index, index] += 2 * shear
        elastic[index + 3, index + 3] = shear
    points = [0.5 - 0.5 / math.sqrt(3.0), 0.5 + 0.5 / math.sqrt(3.0)]
    result = np.zeros((24, 24))
    for point_s in points:
        for point_t in points:
            for point_r in points:
                strain = np.zeros((6, 24))
                for index, corner in enumerate(corner_list()):
                    factor_x = point_s if corner[0] else 1 - point_s
                    factor_y = point_t if corner[1] else 1 - point_t
                    factor_z = point_r if corner[2] else 1 - point_r
                    slope_x = (2 * corner[0] - 1) * factor_y * factor_z
                    slope_y = factor_x * (2 * corner[1] - 1) * factor_z
                    slope_z = factor_x * factor_y * (2 * corner[2] - 1)
                    column = 3 * index
                    strain[0, column] = slope_x
                    strain[1, column + 1] = slope_y
                    strain[2, column + 2] = slope_z
                    strain[3, column] = slope_y
                    strain[3, column + 1] = slope_x
                    strain[4, column + 1] = slope_z
                    strain[4, column + 2] = slope_y
                    strain[5, column] = slope_z
                    strain[5, column + 2] = slope_x
                result += 0.125 * strain.T @ elastic @ strain
    return result


def modal_matrix():
    pair = np.array([[1.0, 1.0], [-1.0, 1.0]])
    change = np.kron(np.kron(np.kron(pair, pair), pair), np.eye(3))
    back = np.linalg.inv(change)
    modal = back.T @ element_matrix() @ back
    rows = []
    for row in range(24):
        rows.append([(col, float(modal[row, col])) for col in range(24) if abs(modal[row, col]) > 1e-9])
    return rows


MODAL = modal_matrix()
DIAG = float(element_matrix()[0, 0])

DEN, PAS, FR, U, LD, PR = 0, 1, 2, 3, 6, 9
FIELDS = 12

MSG = {
    (0, 1): [(DEN, -4, 4), (PAS, -2, 2), (FR, -1, 1), (LD, -1, 1)],
    (0, -1): [(DEN, N, 4), (PAS, N, 2), (FR, N, 2)],
    (1, 1): [(U + c, -2, 2) for c in range(3)] + [(LD + 1, -1, 1), (LD + 2, -1, 1)],
    (1, -1): [(U + c, N, 3) for c in range(3)] + [(LD + c, N, 2) for c in range(3)],
    (2, -1): [(PR + c, N, 1) for c in range(3)],
    (3, 1): [(c, -2, 2) for c in range(3)],
    (3, -1): [(c, N, 2) for c in range(3)],
}
DIAG_ROWS = {
    (0, 1): (4, 4), (0, -1): (0, 4),
    (1, 1): (6, 2), (1, -1): (0, 3),
    (2, -1): (0, 1),
    (3, 1): (6, 2), (3, -1): (0, 2),
}


def units(msg, way):
    return sum(count for _, _, count in MSG[msg, way])


def pad8(count):
    return (count + 7) // 8 * 8


def routes():
    found = []
    for msg in range(4):
        for dx in (-1, 0, 1):
            for dy in (-1, 0, 1):
                if (dx, dy) == (0, 0):
                    continue
                if (dx and (msg, dx) not in MSG) or (dy and (msg, dy) not in MSG):
                    continue
                found.append((msg, dx, dy))
    return found


ROUTES = routes()
STAGES = [(msg, axis, way) for (msg, way) in MSG for axis in (0, 1)]


def stage_shape(msg, axis, way):
    if axis == 0:
        return (units(msg, way), N, NZ)
    return (N, pad8(units(msg, way)), NZ)


def route_shape(msg, dx, dy):
    if dy == 0:
        return stage_shape(msg, 0, dx)
    if dx == 0:
        return stage_shape(msg, 1, dy)
    return (DIAG_ROWS[msg, dx][1], pad8(units(msg, dy)), NZ)


def zshift(value, amount):
    lane = lax.broadcasted_iota(jnp.int32, value.shape, value.ndim - 1)
    moved = pltpu.roll(value, (-amount) % NZ, value.ndim - 1)
    keep = (lane < NZ - amount) if amount > 0 else (lane >= -amount)
    return jnp.where(keep, moved, 0.0)


def yshift(value, amount):
    return pltpu.roll(value, (-amount) % value.shape[-2], value.ndim - 2)


def filter_row(rows):
    across = [rows[2], rows[1] + rows[3], rows[0] + rows[4]]
    total = None
    for dz in range(3):
        plane = None
        for dy in range(3):
            part = None
            for dx in range(3):
                square = dx * dx + dy * dy + dz * dz
                if square < 9:
                    term = (RMIN - math.sqrt(square)) * across[dx]
                    part = term if part is None else part + term
            if part is None:
                continue
            if dy:
                part = yshift(part, dy) + yshift(part, -dy)
            plane = part if plane is None else plane + part
        if dz:
            plane = zshift(plane, dz) + zshift(plane, -dz)
        total = plane if total is None else total + plane
    return total


def transform(value):
    up = zshift(value, 1)
    out = [value + up, up - value]
    ups = [yshift(v, 1) for v in out]
    return [out[0] + ups[0], out[1] + ups[1], ups[0] - out[0], ups[1] - out[1]]


def put_transform(held, row, values):
    for c in range(3):
        for k, value in enumerate(transform(values[c])):
            held[4 * c + k, row] = value


def modes(held, row, part=slice(None)):
    out = [None] * 24
    for c in range(3):
        for k in range(4):
            low, high = held[4 * c + k, row, part, :], held[4 * c + k, row + 1, part, :]
            out[3 * k + c] = low + high
            out[12 + 3 * k + c] = high - low
    return out


def stress(mode):
    out = []
    for row in MODAL:
        total = None
        for col, weight in row:
            term = weight * mode[col]
            total = term if total is None else total + term
        out.append(total)
    return out


def dot_modes(first, second):
    total = None
    for a, b in zip(first, second):
        if b is not None:
            total = a * b if total is None else total + a * b
    return total


def spread_forces(held, work, stiff, low, high):
    for k in range(12):
        work[k, low] = jnp.zeros((L, NZ), jnp.float32)

    def step(row, carry):
        scale = stiff[row]
        force = stress(modes(held, row))
        for c in range(3):
            for k in range(4):
                even, odd = force[3 * k + c], force[12 + 3 * k + c]
                odd = odd * scale
                slot = 4 * c + k
                if even is None:
                    work[slot, row] = work[slot, row] - odd
                    work[slot, row + 1] = odd
                else:
                    even = even * scale
                    work[slot, row] = work[slot, row] + (even - odd)
                    work[slot, row + 1] = even + odd
        return carry

    lax.fori_loop(low, high, step, 0)


def node_forces(work, row, c):
    out = []
    for z in range(2):
        even, odd = work[4 * c + z, row], work[4 * c + 2 + z, row]
        out.append((even - odd) + yshift(even + odd, -1))
    return (out[0] - out[1]) + zshift(out[0] + out[1], -1)


def kernel(size_x, size_y, *refs):
    inputs, refs = refs[:7], refs[7:]
    density, passive, fixed, load_nodes, port, guess, primal = inputs
    (sens, adjoint), refs = refs[:2], refs[2:]
    stages, refs = dict(zip(STAGES, refs)), refs[len(STAGES):]
    lands, refs = dict(zip(ROUTES, refs)), refs[len(ROUTES):]
    (ext, mask, weight, phys, slope, stiff, factor, res_z, q, inv, tu, td, tq, tp, work, sp,
     red1, red2, acc, send_sem, recv_sem, red_send, red_recv) = refs
    gx, gy = lax.axis_index("gx"), lax.axis_index("gy")
    lower = 4
    upper = size_x // lower * size_y
    group, rank = gx // lower, gx % lower
    upper_rank = group * size_y + gy

    def there(dx, dy):
        ok = None
        for pos, size, d in ((gx, size_x, dx), (gy, size_y, dy)):
            if d:
                this = (pos + d >= 0) & (pos + d < size)
                ok = this if ok is None else ok & this
        return ok

    def peer1(k):
        return (group * lower + (rank + k) % lower, gy)

    def peer2(k):
        other = (upper_rank + k) % upper
        return ((other // size_y) * lower + rank, other % size_y)

    barrier = pltpu.get_barrier_semaphore()
    expected = jnp.int32(lower - 1 + upper - 1)
    for dx in (-1, 0, 1):
        for dy in (-1, 0, 1):
            if (dx, dy) != (0, 0):
                ok = there(dx, dy)
                expected = expected + ok.astype(jnp.int32)

                @pl.when(ok)
                def _():
                    pl.semaphore_signal(barrier, inc=1, device_id=(gx + dx, gy + dy), device_id_type=MESH)
    for k in range(1, lower):
        pl.semaphore_signal(barrier, inc=1, device_id=peer1(k), device_id_type=MESH)
    for k in range(1, upper):
        pl.semaphore_signal(barrier, inc=1, device_id=peer2(k), device_id_type=MESH)

    own = slice(W, W + N)
    for f in range(FIELDS):
        def clear(i, carry):
            ext[f, i] = jnp.zeros((L, NZ), jnp.float32)
            return carry
        lax.fori_loop(0, L, clear, 0)

    def fill(i, carry):
        free = (1 - fixed[i]).astype(jnp.float32)
        solid = passive[i] == 1
        loaded = free * load_nodes[i].astype(jnp.float32)
        ext[DEN, W + i, own, :] = jnp.where(solid, 1.0, density[i])
        ext[PAS, W + i, own, :] = passive[i].astype(jnp.float32)
        ext[FR, W + i, own, :] = free
        for c in range(3):
            ext[U + c, W + i, own, :] = free * guess[c, i]
            ext[LD + c, W + i, own, :] = loaded * port[c, i]
            ext[PR + c, W + i, own, :] = free * primal[c, i]
        return carry

    lax.fori_loop(0, N, fill, 0)

    def pack(msg, source):
        for way in (1, -1):
            if (msg, way) not in MSG:
                continue
            flat_x, flat_y = stages[msg, 0, way], stages[msg, 1, way]
            at = 0
            for f, first, count in MSG[msg, way]:
                start = W + (first + N if way == 1 else first - N)
                flat_x[at:at + count] = source[f, start:start + count, own, :]
                flat_y[:, at:at + count, :] = source[f, own, start:start + count, :]
                at += count
            if at < flat_y.shape[1]:
                flat_y[:, at:, :] = jnp.zeros((N, flat_y.shape[1] - at, NZ), jnp.float32)

    def copy(route):
        msg, dx, dy = route
        at = ROUTES.index(route)
        if dy == 0:
            source = stages[msg, 0, dx]
        elif dx == 0:
            source = stages[msg, 1, dy]
        else:
            first, count = DIAG_ROWS[msg, dx]
            source = stages[msg, 1, dy].at[first:first + count]
        return pltpu.make_async_remote_copy(
            src_ref=source,
            dst_ref=lands[route],
            send_sem=send_sem.at[at],
            recv_sem=recv_sem.at[at],
            device_id=(gx + dx, gy + dy),
            device_id_type=MESH,
        )

    def send(msg):
        for route in ROUTES:
            if route[0] == msg:
                @pl.when(there(route[1], route[2]))
                def _():
                    copy(route).start()

    def receive(msg, target):
        for route in ROUTES:
            if route[0] != msg:
                continue
            _, dx, dy = route

            @pl.when(there(-dx, -dy))
            def _():
                copy(route).wait_recv()
                land = lands[route]
                at = 0
                for f, first, count in MSG[msg, dy if dy else dx]:
                    begin = W + first
                    if dy == 0:
                        target[f, begin:begin + count, own, :] = land[at:at + count]
                    elif dx == 0:
                        target[f, own, begin:begin + count, :] = land[:, at:at + count, :]
                    else:
                        source, rows = DIAG_ROWS[msg, dx]
                        row = W + (source - N if dx == 1 else source + N)
                        target[f, row:row + rows, begin:begin + count, :] = land[:, at:at + count, :]
                    at += count

    def finish(msg):
        for route in ROUTES:
            if route[0] == msg:
                @pl.when(there(route[1], route[2]))
                def _():
                    copy(route).wait_send()

    pack(0, ext)
    pl.semaphore_wait(barrier, expected)
    send(0)
    pack(1, ext)
    send(1)
    pack(2, ext)
    send(2)

    sub = lax.broadcasted_iota(jnp.int32, (L, NZ), 0)
    at_y = gy * N - W + sub
    inside_y = ((at_y >= 0) & (at_y < size_y * N)).astype(jnp.float32)
    owned = ((sub >= W) & (sub < W + N)).astype(jnp.float32)

    def inside_x(i):
        at_x = gx * N - W + i
        return ((at_x >= 0) & (at_x < size_x * N)).astype(jnp.float32)

    def weigh(i, carry):
        total = filter_row([inside_x(i + d) * inside_y for d in range(-2, 3)])
        weight[i] = 1.0 / jnp.where(total > 0.0, total, 1.0)
        return carry

    lax.fori_loop(2, 14, weigh, 0)

    receive(0, ext)
    denom = 2.0 * math.tanh(BETA * ETA)

    def densities(i, carry):
        filtered = filter_row([ext[DEN, i + d] for d in range(-2, 3)]) * weight[i]
        bent = jnp.tanh(BETA * (filtered - ETA))
        solid = ext[PAS, i]
        physical = jnp.where(solid == 1.0, 1.0, (math.tanh(BETA * ETA) + bent) / denom)
        square = physical * physical
        stiff[i] = (EMIN + (1.0 - EMIN) * (square * physical)) * (inside_x(i) * inside_y)
        gain = BETA * (1.0 - bent * bent) / denom
        factor[i] = (-3.0 * (1.0 - EMIN)) * square * gain * (1.0 - solid) * weight[i]
        return carry

    lax.fori_loop(2, 14, densities, 0)

    receive(1, ext)

    def load_u(i, carry):
        put_transform(tu, i, [ext[U + c, i] for c in range(3)])
        return carry

    lax.fori_loop(2, 15, load_u, 0)
    spread_forces(tu, work, stiff, 2, 14)
    acc[...] = jnp.zeros_like(acc)

    def is_owned(i):
        return ((i >= W) & (i < W + N)).astype(jnp.float32) * owned

    def residuals(i, carry):
        free = ext[FR, i]
        pair = stiff[i] + stiff[i - 1]
        pair = pair + yshift(pair, -1)
        total = DIAG * (pair + zshift(pair, -1))
        inverse = free / jnp.where(total > 0.0, total, 1.0)
        inv[i] = inverse
        dot = None
        values = []
        for c in range(3):
            residual = ext[LD + c, i] - free * node_forces(work, i, c)
            value = inverse * residual
            res_z[c, i] = value
            values.append(value)
            dot = residual * value if dot is None else dot + residual * value
        put_transform(td, i, values)
        acc[0] = acc[0] + is_owned(i) * dot
        return carry

    lax.fori_loop(3, 14, residuals, 0)
    spread_forces(td, work, stiff, 3, 13)

    def images(i, carry):
        free, inverse = ext[FR, i], inv[i]
        dot_w = dot_q = None
        values = []
        for c in range(3):
            image = free * node_forces(work, i, c)
            value = inverse * image
            q[c, i] = value
            values.append(value)
            first, second = image * res_z[c, i], image * value
            dot_w = first if dot_w is None else dot_w + first
            dot_q = second if dot_q is None else dot_q + second
        put_transform(tq, i, values)
        acc[1] = acc[1] + is_owned(i) * dot_w
        acc[2] = acc[2] + is_owned(i) * dot_q
        return carry

    lax.fori_loop(4, 13, images, 0)

    def curvature(i, total):
        mode = modes(tq, i, own)
        return total + stiff[i, own, :] * dot_modes(mode, stress(mode))

    last = lax.fori_loop(W, W + N, curvature, jnp.zeros((N, NZ), jnp.float32))

    parts = []
    for value in (acc[0], acc[1], acc[2], last):
        line = jnp.sum(value, axis=0, keepdims=True)
        parts.append(line[:, :128] + line[:, 128:])
    for k, part in enumerate(parts):
        red1[0, k:k + 1, :] = part
    red1[0, 4:8, :] = jnp.zeros((4, 128), jnp.float32)

    def reduce_copy(buf, k, base, target):
        return pltpu.make_async_remote_copy(
            src_ref=buf.at[0],
            dst_ref=buf.at[k],
            send_sem=red_send.at[base + k],
            recv_sem=red_recv.at[base + k],
            device_id=target,
            device_id_type=MESH,
        )

    first_copies = [reduce_copy(red1, k, 0, peer1(k)) for k in range(1, lower)]
    for item in first_copies:
        item.start()

    receive(2, ext)

    def load_p(i, carry):
        put_transform(tp, i, [ext[PR + c, i] for c in range(3)])
        return carry

    lax.fori_loop(4, 13, load_p, 0)

    for item in first_copies:
        item.wait_recv()
    total = red1[0]
    for k in range(1, lower):
        total = total + red1[k]
    red2[0] = total
    second_copies = [reduce_copy(red2, k, lower, peer2(k)) for k in range(1, upper)]
    for item in second_copies:
        item.start()

    for c in range(3):
        def clear_sp(i, carry):
            sp[c, i] = jnp.zeros((L, NZ), jnp.float32)
            return carry
        lax.fori_loop(2, 14, clear_sp, 0)

    def energies(i, carry):
        force = stress(modes(tp, i, own))
        scale = factor[i, own, :]
        for k, held in enumerate((tu, td, tq)):
            sp[k, i, own, :] = scale * dot_modes(modes(held, i, own), force)
        return carry

    lax.fori_loop(W, W + N, energies, 0)
    pack(3, sp)
    send(3)
    receive(3, sp)

    for item in second_copies:
        item.wait_recv()
    total = red2[0]
    for k in range(1, upper):
        total = total + red2[k]
    rz, dw, wq, qv = [jnp.sum(total[k:k + 1, :], axis=1, keepdims=True) for k in range(4)]
    alpha = rz / dw
    after = alpha * alpha * wq - rz
    grow = 1.0 + after / rz
    curve = grow * grow * dw - 2.0 * alpha * grow * wq + alpha * alpha * qv
    beyond = after / curve
    coef_d = alpha + beyond * grow
    coef_q = -beyond * alpha

    def join(i, carry):
        mask[i] = sp[0, i] + coef_d * sp[1, i] + coef_q * sp[2, i]
        return carry

    lax.fori_loop(2, 14, join, 0)

    def result(i, carry):
        row = W + i
        value = filter_row([mask[row + d] for d in range(-2, 3)])
        mine = (1.0 - ext[PAS, row]) * value
        sens[i] = mine[own]
        for c in range(3):
            adjoint[c, i] = (ext[U + c, row, own, :] + coef_d * res_z[c, row, own, :]
                             + coef_q * q[c, row, own, :])
        return carry

    lax.fori_loop(0, N, result, 0)
    for msg in range(4):
        finish(msg)
    for item in first_copies + second_copies:
        item.wait_send()


def local(size_x, size_y, *arrays):
    f32 = jnp.float32
    upper = size_x // 4 * size_y
    scratch = [pltpu.VMEM(stage_shape(*stage), f32) for stage in STAGES]
    scratch += [pltpu.VMEM(route_shape(*route), f32) for route in ROUTES]
    plain = pltpu.VMEM((L, L, NZ), f32)
    three = pltpu.VMEM((3, L, L, NZ), f32)
    twelve = pltpu.VMEM((12, L, L, NZ), f32)
    scratch += [twelve, plain, plain, plain, plain, plain, plain, three, three, plain]
    scratch += [twelve] * 5 + [three]
    scratch += [
        pltpu.VMEM((4, 8, 128), f32),
        pltpu.VMEM((upper, 8, 128), f32),
        pltpu.VMEM((3, L, NZ), f32),
        pltpu.SemaphoreType.DMA((len(ROUTES),)),
        pltpu.SemaphoreType.DMA((len(ROUTES),)),
        pltpu.SemaphoreType.DMA((4 + upper,)),
        pltpu.SemaphoreType.DMA((4 + upper,)),
    ]
    vmem = pl.BlockSpec(memory_space=pltpu.VMEM)
    return pl.pallas_call(
        lambda *refs: kernel(size_x, size_y, *refs),
        out_shape=(
            jax.ShapeDtypeStruct((N, N, NZ), f32),
            jax.ShapeDtypeStruct((3, N, N, NZ), f32),
        ),
        in_specs=[vmem] * 7,
        out_specs=(vmem, vmem),
        scratch_shapes=scratch,
        compiler_params=pltpu.CompilerParams(
            collective_id=0, has_side_effects=True, vmem_limit_bytes=48 * 1024 * 1024
        ),
    )(*arrays)


def solution(mesh):
    grid = P("gx", "gy", None)
    field = P(None, "gx", "gy", None)
    size_x, size_y = mesh.shape["gx"], mesh.shape["gy"]
    return jax.shard_map(
        lambda *arrays: local(size_x, size_y, *arrays),
        mesh=mesh,
        in_specs=(grid, grid, grid, grid, field, field, field),
        out_specs=(grid, field),
        check_vma=False,
    )
```

```python
import math

import jax
import jax.numpy as jnp
import numpy as np
from jax import lax
from jax.experimental import pallas as pl
from jax.experimental.pallas import tpu as pltpu
from jax.sharding import PartitionSpec as P

EMIN = 0.01
BETA = 4.0
ETA = 0.5
RMIN = 3.0
N = 8
W = 4
L = N + 2 * W
NZ = 256
MESH = pl.DeviceIdType.MESH


def corner_list():
    return [
        (along_x, along_y, along_z)
        for along_x in (0, 1)
        for along_y in (0, 1)
        for along_z in (0, 1)
    ]


def element_matrix():
    poisson = 0.3
    lame = poisson / ((1 + poisson) * (1 - 2 * poisson))
    shear = 0.5 / (1 + poisson)
    elastic = np.zeros((6, 6))
    elastic[:3, :3] = lame
    for index in range(3):
        elastic[index, index] += 2 * shear
        elastic[index + 3, index + 3] = shear
    points = [0.5 - 0.5 / math.sqrt(3.0), 0.5 + 0.5 / math.sqrt(3.0)]
    result = np.zeros((24, 24))
    for point_s in points:
        for point_t in points:
            for point_r in points:
                strain = np.zeros((6, 24))
                for index, corner in enumerate(corner_list()):
                    factor_x = point_s if corner[0] else 1 - point_s
                    factor_y = point_t if corner[1] else 1 - point_t
                    factor_z = point_r if corner[2] else 1 - point_r
                    slope_x = (2 * corner[0] - 1) * factor_y * factor_z
                    slope_y = factor_x * (2 * corner[1] - 1) * factor_z
                    slope_z = factor_x * factor_y * (2 * corner[2] - 1)
                    column = 3 * index
                    strain[0, column] = slope_x
                    strain[1, column + 1] = slope_y
                    strain[2, column + 2] = slope_z
                    strain[3, column] = slope_y
                    strain[3, column + 1] = slope_x
                    strain[4, column + 1] = slope_z
                    strain[4, column + 2] = slope_y
                    strain[5, column] = slope_z
                    strain[5, column + 2] = slope_x
                result += 0.125 * strain.T @ elastic @ strain
    return result


def modal_matrix():
    pair = np.array([[1.0, 1.0], [-1.0, 1.0]])
    change = np.kron(np.kron(np.kron(pair, pair), pair), np.eye(3))
    back = np.linalg.inv(change)
    modal = back.T @ element_matrix() @ back
    rows = []
    for row in range(24):
        rows.append([(col, float(modal[row, col])) for col in range(24) if abs(modal[row, col]) > 1e-9])
    return rows


MODAL = modal_matrix()
DIAG = float(element_matrix()[0, 0])

DEN, PAS, FR, U, LD, PR = 0, 1, 2, 3, 6, 9
FIELDS = 12

MSG = {
    (0, 1): [(DEN, -4, 4), (PAS, -2, 2), (FR, -1, 1), (LD, -1, 1)],
    (0, -1): [(DEN, N, 4), (PAS, N, 2), (FR, N, 2)],
    (1, 1): [(U + c, -2, 2) for c in range(3)] + [(LD + 1, -1, 1), (LD + 2, -1, 1)],
    (1, -1): [(U + c, N, 3) for c in range(3)] + [(LD + c, N, 2) for c in range(3)],
    (2, -1): [(PR + c, N, 1) for c in range(3)],
    (3, 1): [(c, -2, 2) for c in range(3)],
    (3, -1): [(c, N, 2) for c in range(3)],
}
DIAG_ROWS = {
    (0, 1): (4, 4), (0, -1): (0, 4),
    (1, 1): (6, 2), (1, -1): (0, 3),
    (2, -1): (0, 1),
    (3, 1): (6, 2), (3, -1): (0, 2),
}


def units(msg, way):
    return sum(count for _, _, count in MSG[msg, way])


def pad8(count):
    return (count + 7) // 8 * 8


def routes():
    found = []
    for msg in range(4):
        for dx in (-1, 0, 1):
            for dy in (-1, 0, 1):
                if (dx, dy) == (0, 0):
                    continue
                if (dx and (msg, dx) not in MSG) or (dy and (msg, dy) not in MSG):
                    continue
                found.append((msg, dx, dy))
    return found


ROUTES = routes()
STAGES = [(msg, axis, way) for (msg, way) in MSG for axis in (0, 1)]


def stage_shape(msg, axis, way):
    if axis == 0:
        return (units(msg, way), N, NZ)
    return (N, pad8(units(msg, way)), NZ)


def route_shape(msg, dx, dy):
    if dy == 0:
        return stage_shape(msg, 0, dx)
    if dx == 0:
        return stage_shape(msg, 1, dy)
    return (DIAG_ROWS[msg, dx][1], pad8(units(msg, dy)), NZ)


def zshift(value, amount):
    lane = lax.broadcasted_iota(jnp.int32, value.shape, value.ndim - 1)
    moved = pltpu.roll(value, (-amount) % NZ, value.ndim - 1)
    keep = (lane < NZ - amount) if amount > 0 else (lane >= -amount)
    return jnp.where(keep, moved, 0.0)


def yshift(value, amount):
    return pltpu.roll(value, (-amount) % value.shape[-2], value.ndim - 2)


def filter_row(rows):
    across = [rows[2], rows[1] + rows[3], rows[0] + rows[4]]
    total = None
    for dz in range(3):
        plane = None
        for dy in range(3):
            part = None
            for dx in range(3):
                square = dx * dx + dy * dy + dz * dz
                if square < 9:
                    term = (RMIN - math.sqrt(square)) * across[dx]
                    part = term if part is None else part + term
            if part is None:
                continue
            if dy:
                part = yshift(part, dy) + yshift(part, -dy)
            plane = part if plane is None else plane + part
        if dz:
            plane = zshift(plane, dz) + zshift(plane, -dz)
        total = plane if total is None else total + plane
    return total


def transform(value):
    up = zshift(value, 1)
    out = [value + up, up - value]
    ups = [yshift(v, 1) for v in out]
    return [out[0] + ups[0], out[1] + ups[1], ups[0] - out[0], ups[1] - out[1]]


def put_transform(held, row, values):
    for c in range(3):
        for k, value in enumerate(transform(values[c])):
            held[4 * c + k, row] = value


def modes(held, row, part=slice(None)):
    out = [None] * 24
    for c in range(3):
        for k in range(4):
            low, high = held[4 * c + k, row, part, :], held[4 * c + k, row + 1, part, :]
            out[3 * k + c] = low + high
            out[12 + 3 * k + c] = high - low
    return out


def stress(mode):
    out = []
    for row in MODAL:
        total = None
        for col, weight in row:
            term = weight * mode[col]
            total = term if total is None else total + term
        out.append(total)
    return out


def dot_modes(first, second):
    total = None
    for a, b in zip(first, second):
        if b is not None:
            total = a * b if total is None else total + a * b
    return total


def spread_forces(held, work, stiff, low, high):
    for k in range(12):
        work[k, low] = jnp.zeros((L, NZ), jnp.float32)

    def step(row, carry):
        scale = stiff[row]
        force = stress(modes(held, row))
        for c in range(3):
            for k in range(4):
                even, odd = force[3 * k + c], force[12 + 3 * k + c]
                odd = odd * scale
                slot = 4 * c + k
                if even is None:
                    work[slot, row] = work[slot, row] - odd
                    work[slot, row + 1] = odd
                else:
                    even = even * scale
                    work[slot, row] = work[slot, row] + (even - odd)
                    work[slot, row + 1] = even + odd
        return carry

    lax.fori_loop(low, high, step, 0)


def node_forces(work, row, c):
    out = []
    for z in range(2):
        even, odd = work[4 * c + z, row], work[4 * c + 2 + z, row]
        out.append((even - odd) + yshift(even + odd, -1))
    return (out[0] - out[1]) + zshift(out[0] + out[1], -1)


def kernel(size_x, size_y, *refs):
    inputs, refs = refs[:7], refs[7:]
    (sens, adjoint), refs = refs[:2], refs[2:]
    held, refs = refs[:7], refs[7:]
    density, passive, fixed, load_nodes, port, guess, primal = held
    stages, refs = dict(zip(STAGES, refs)), refs[len(STAGES):]
    lands, refs = dict(zip(ROUTES, refs)), refs[len(ROUTES):]
    (ext, mask, weight, phys, slope, stiff, factor, res_z, q, inv, tu, td, tq, tp, work, sp,
     red1, red2, acc, send_sem, recv_sem, red_send, red_recv, in_sem) = refs
    loads = [pltpu.make_async_copy(a, b, in_sem.at[k]) for k, (a, b) in enumerate(zip(inputs, held))]
    for item in loads:
        item.start()
    gx, gy = lax.axis_index("gx"), lax.axis_index("gy")
    lower = 4
    upper = size_x // lower * size_y
    group, rank = gx // lower, gx % lower
    upper_rank = group * size_y + gy

    def there(dx, dy):
        ok = None
        for pos, size, d in ((gx, size_x, dx), (gy, size_y, dy)):
            if d:
                this = (pos + d >= 0) & (pos + d < size)
                ok = this if ok is None else ok & this
        return ok

    def peer1(k):
        return (group * lower + (rank + k) % lower, gy)

    def peer2(k):
        other = (upper_rank + k) % upper
        return ((other // size_y) * lower + rank, other % size_y)

    barrier = pltpu.get_barrier_semaphore()
    expected = jnp.int32(lower - 1 + upper - 1)
    for dx in (-1, 0, 1):
        for dy in (-1, 0, 1):
            if (dx, dy) != (0, 0):
                ok = there(dx, dy)
                expected = expected + ok.astype(jnp.int32)

                @pl.when(ok)
                def _():
                    pl.semaphore_signal(barrier, inc=1, device_id=(gx + dx, gy + dy), device_id_type=MESH)
    for k in range(1, lower):
        pl.semaphore_signal(barrier, inc=1, device_id=peer1(k), device_id_type=MESH)
    for k in range(1, upper):
        pl.semaphore_signal(barrier, inc=1, device_id=peer2(k), device_id_type=MESH)

    sub = lax.broadcasted_iota(jnp.int32, (L, NZ), 0)
    at_y = gy * N - W + sub
    inside_y = ((at_y >= 0) & (at_y < size_y * N)).astype(jnp.float32)
    owned = ((sub >= W) & (sub < W + N)).astype(jnp.float32)

    def inside_x(i):
        at_x = gx * N - W + i
        return ((at_x >= 0) & (at_x < size_x * N)).astype(jnp.float32)

    def weigh(i, carry):
        total = filter_row([inside_x(i + d) * inside_y for d in range(-2, 3)])
        weight[i] = 1.0 / jnp.where(total > 0.0, total, 1.0)
        return carry

    lax.fori_loop(2, 14, weigh, 0)

    own = slice(W, W + N)
    def clear(i, carry):
        for f in range(FIELDS):
            ext[f, i] = jnp.zeros((L, NZ), jnp.float32)
        for c in range(3):
            sp[c, i] = jnp.zeros((L, NZ), jnp.float32)
        return carry

    lax.fori_loop(0, L, clear, 0)
    for item in loads:
        item.wait()

    def fill(i, carry):
        free = (1 - fixed[i]).astype(jnp.float32)
        solid = passive[i] == 1
        loaded = free * load_nodes[i].astype(jnp.float32)
        ext[DEN, W + i, own, :] = jnp.where(solid, 1.0, density[i])
        ext[PAS, W + i, own, :] = passive[i].astype(jnp.float32)
        ext[FR, W + i, own, :] = free
        for c in range(3):
            ext[U + c, W + i, own, :] = free * guess[c, i]
            ext[LD + c, W + i, own, :] = loaded * port[c, i]
            ext[PR + c, W + i, own, :] = free * primal[c, i]
        return carry

    lax.fori_loop(0, N, fill, 0)

    def pack(msg, source):
        for way in (1, -1):
            if (msg, way) not in MSG:
                continue
            flat_x, flat_y = stages[msg, 0, way], stages[msg, 1, way]
            at = 0
            for f, first, count in MSG[msg, way]:
                start = W + (first + N if way == 1 else first - N)
                flat_x[at:at + count] = source[f, start:start + count, own, :]
                flat_y[:, at:at + count, :] = source[f, own, start:start + count, :]
                at += count
            if at < flat_y.shape[1]:
                flat_y[:, at:, :] = jnp.zeros((N, flat_y.shape[1] - at, NZ), jnp.float32)

    def copy(route):
        msg, dx, dy = route
        at = ROUTES.index(route)
        if dy == 0:
            source = stages[msg, 0, dx]
        elif dx == 0:
            source = stages[msg, 1, dy]
        else:
            first, count = DIAG_ROWS[msg, dx]
            source = stages[msg, 1, dy].at[first:first + count]
        return pltpu.make_async_remote_copy(
            src_ref=source,
            dst_ref=lands[route],
            send_sem=send_sem.at[at],
            recv_sem=recv_sem.at[at],
            device_id=(gx + dx, gy + dy),
            device_id_type=MESH,
        )

    def send(msg):
        for route in ROUTES:
            if route[0] == msg:
                @pl.when(there(route[1], route[2]))
                def _():
                    copy(route).start()

    def receive(msg, target):
        for route in ROUTES:
            if route[0] != msg:
                continue
            _, dx, dy = route

            @pl.when(there(-dx, -dy))
            def _():
                copy(route).wait_recv()
                land = lands[route]
                at = 0
                for f, first, count in MSG[msg, dy if dy else dx]:
                    begin = W + first
                    if dy == 0:
                        target[f, begin:begin + count, own, :] = land[at:at + count]
                    elif dx == 0:
                        target[f, own, begin:begin + count, :] = land[:, at:at + count, :]
                    else:
                        source, rows = DIAG_ROWS[msg, dx]
                        row = W + (source - N if dx == 1 else source + N)
                        target[f, row:row + rows, begin:begin + count, :] = land[:, at:at + count, :]
                    at += count

    def finish(msg):
        for route in ROUTES:
            if route[0] == msg:
                @pl.when(there(route[1], route[2]))
                def _():
                    copy(route).wait_send()

    pack(0, ext)
    pl.semaphore_wait(barrier, expected)
    send(0)
    pack(1, ext)
    send(1)
    pack(2, ext)
    send(2)

    receive(0, ext)
    denom = 2.0 * math.tanh(BETA * ETA)

    def densities(i, carry):
        filtered = filter_row([ext[DEN, i + d] for d in range(-2, 3)]) * weight[i]
        bent = jnp.tanh(BETA * (filtered - ETA))
        solid = ext[PAS, i]
        physical = jnp.where(solid == 1.0, 1.0, (math.tanh(BETA * ETA) + bent) / denom)
        square = physical * physical
        stiff[i] = (EMIN + (1.0 - EMIN) * (square * physical)) * (inside_x(i) * inside_y)
        gain = BETA * (1.0 - bent * bent) / denom
        factor[i] = (-3.0 * (1.0 - EMIN)) * square * gain * (1.0 - solid) * weight[i]
        return carry

    lax.fori_loop(2, 14, densities, 0)

    receive(1, ext)

    def load_u(i, carry):
        put_transform(tu, i, [ext[U + c, i] for c in range(3)])
        return carry

    lax.fori_loop(2, 15, load_u, 0)
    spread_forces(tu, work, stiff, 2, 14)
    acc[...] = jnp.zeros_like(acc)

    def is_owned(i):
        return ((i >= W) & (i < W + N)).astype(jnp.float32) * owned

    def residuals(i, carry):
        free = ext[FR, i]
        pair = stiff[i] + stiff[i - 1]
        pair = pair + yshift(pair, -1)
        total = DIAG * (pair + zshift(pair, -1))
        inverse = free / jnp.where(total > 0.0, total, 1.0)
        inv[i] = inverse
        dot = None
        values = []
        for c in range(3):
            residual = ext[LD + c, i] - free * node_forces(work, i, c)
            value = inverse * residual
            res_z[c, i] = value
            values.append(value)
            dot = residual * value if dot is None else dot + residual * value
        put_transform(td, i, values)
        acc[0] = acc[0] + is_owned(i) * dot
        return carry

    lax.fori_loop(3, 14, residuals, 0)
    spread_forces(td, work, stiff, 3, 13)

    def images(i, carry):
        free, inverse = ext[FR, i], inv[i]
        dot_w = dot_q = None
        values = []
        for c in range(3):
            image = free * node_forces(work, i, c)
            value = inverse * image
            q[c, i] = value
            values.append(value)
            first, second = image * res_z[c, i], image * value
            dot_w = first if dot_w is None else dot_w + first
            dot_q = second if dot_q is None else dot_q + second
        put_transform(tq, i, values)
        acc[1] = acc[1] + is_owned(i) * dot_w
        acc[2] = acc[2] + is_owned(i) * dot_q
        return carry

    lax.fori_loop(4, 13, images, 0)

    def curvature(i, total):
        mode = modes(tq, i, own)
        return total + stiff[i, own, :] * dot_modes(mode, stress(mode))

    last = lax.fori_loop(W, W + N, curvature, jnp.zeros((N, NZ), jnp.float32))

    parts = []
    for value in (acc[0], acc[1], acc[2], last):
        line = jnp.sum(value, axis=0, keepdims=True)
        parts.append(line[:, :128] + line[:, 128:])
    for k, part in enumerate(parts):
        red1[0, k:k + 1, :] = part
    red1[0, 4:8, :] = jnp.zeros((4, 128), jnp.float32)

    def reduce_copy(buf, k, base, target):
        return pltpu.make_async_remote_copy(
            src_ref=buf.at[0],
            dst_ref=buf.at[k],
            send_sem=red_send.at[base + k],
            recv_sem=red_recv.at[base + k],
            device_id=target,
            device_id_type=MESH,
        )

    first_copies = [reduce_copy(red1, k, 0, peer1(k)) for k in range(1, lower)]
    for item in first_copies:
        item.start()

    receive(2, ext)

    def load_p(i, carry):
        put_transform(tp, i, [ext[PR + c, i] for c in range(3)])
        return carry

    lax.fori_loop(4, 13, load_p, 0)

    for item in first_copies:
        item.wait_recv()
    total = red1[0]
    for k in range(1, lower):
        total = total + red1[k]
    red2[0] = total
    second_copies = [reduce_copy(red2, k, lower, peer2(k)) for k in range(1, upper)]
    for item in second_copies:
        item.start()

    def energies(i, carry):
        force = stress(modes(tp, i, own))
        scale = factor[i, own, :]
        for k, held in enumerate((tu, td, tq)):
            sp[k, i, own, :] = scale * dot_modes(modes(held, i, own), force)
        return carry

    lax.fori_loop(W, W + N, energies, 0)
    pack(3, sp)
    send(3)
    receive(3, sp)

    for item in second_copies:
        item.wait_recv()
    total = red2[0]
    for k in range(1, upper):
        total = total + red2[k]
    rz, dw, wq, qv = [jnp.sum(total[k:k + 1, :], axis=1, keepdims=True) for k in range(4)]
    alpha = rz / dw
    after = alpha * alpha * wq - rz
    grow = 1.0 + after / rz
    curve = grow * grow * dw - 2.0 * alpha * grow * wq + alpha * alpha * qv
    beyond = after / curve
    coef_d = alpha + beyond * grow
    coef_q = -beyond * alpha

    def join(i, carry):
        mask[i] = sp[0, i] + coef_d * sp[1, i] + coef_q * sp[2, i]
        return carry

    lax.fori_loop(2, 14, join, 0)

    def result(i, carry):
        row = W + i
        value = filter_row([mask[row + d] for d in range(-2, 3)])
        mine = (1.0 - ext[PAS, row]) * value
        sens[i] = mine[own]
        for c in range(3):
            adjoint[c, i] = (ext[U + c, row, own, :] + coef_d * res_z[c, row, own, :]
                             + coef_q * q[c, row, own, :])
        return carry

    lax.fori_loop(0, N, result, 0)
    for msg in range(4):
        finish(msg)
    for item in first_copies + second_copies:
        item.wait_send()


def local(size_x, size_y, *arrays):
    f32 = jnp.float32
    upper = size_x // 4 * size_y
    scratch = [pltpu.VMEM(array.shape, array.dtype) for array in arrays]
    scratch += [pltpu.VMEM(stage_shape(*stage), f32) for stage in STAGES]
    scratch += [pltpu.VMEM(route_shape(*route), f32) for route in ROUTES]
    plain = pltpu.VMEM((L, L, NZ), f32)
    three = pltpu.VMEM((3, L, L, NZ), f32)
    twelve = pltpu.VMEM((12, L, L, NZ), f32)
    scratch += [twelve, plain, plain, plain, plain, plain, plain, three, three, plain]
    scratch += [twelve] * 5 + [three]
    scratch += [
        pltpu.VMEM((4, 8, 128), f32),
        pltpu.VMEM((upper, 8, 128), f32),
        pltpu.VMEM((3, L, NZ), f32),
        pltpu.SemaphoreType.DMA((len(ROUTES),)),
        pltpu.SemaphoreType.DMA((len(ROUTES),)),
        pltpu.SemaphoreType.DMA((4 + upper,)),
        pltpu.SemaphoreType.DMA((4 + upper,)),
        pltpu.SemaphoreType.DMA((7,)),
    ]
    vmem = pl.BlockSpec(memory_space=pltpu.VMEM)
    return pl.pallas_call(
        lambda *refs: kernel(size_x, size_y, *refs),
        out_shape=(
            jax.ShapeDtypeStruct((N, N, NZ), f32),
            jax.ShapeDtypeStruct((3, N, N, NZ), f32),
        ),
        in_specs=[pl.BlockSpec(memory_space=pltpu.HBM)] * 7,
        out_specs=(vmem, vmem),
        scratch_shapes=scratch,
        compiler_params=pltpu.CompilerParams(
            collective_id=0, has_side_effects=True, vmem_limit_bytes=65000 * 1024
        ),
    )(*arrays)


def solution(mesh):
    grid = P("gx", "gy", None)
    field = P(None, "gx", "gy", None)
    size_x, size_y = mesh.shape["gx"], mesh.shape["gy"]
    return jax.shard_map(
        lambda *arrays: local(size_x, size_y, *arrays),
        mesh=mesh,
        in_specs=(grid, grid, grid, grid, field, field, field),
        out_specs=(grid, field),
        check_vma=False,
    )
```

```python
import math

import jax
import jax.numpy as jnp
import numpy as np
from jax import lax
from jax.experimental import pallas as pl
from jax.experimental.pallas import tpu as pltpu
from jax.sharding import PartitionSpec as P

EMIN = 0.01
BETA = 4.0
ETA = 0.5
RMIN = 3.0
N = 8
W = 4
L = N + 2 * W
NZ = 256
MESH = pl.DeviceIdType.MESH


def corner_list():
    return [
        (along_x, along_y, along_z)
        for along_x in (0, 1)
        for along_y in (0, 1)
        for along_z in (0, 1)
    ]


def element_matrix():
    poisson = 0.3
    lame = poisson / ((1 + poisson) * (1 - 2 * poisson))
    shear = 0.5 / (1 + poisson)
    elastic = np.zeros((6, 6))
    elastic[:3, :3] = lame
    for index in range(3):
        elastic[index, index] += 2 * shear
        elastic[index + 3, index + 3] = shear
    points = [0.5 - 0.5 / math.sqrt(3.0), 0.5 + 0.5 / math.sqrt(3.0)]
    result = np.zeros((24, 24))
    for point_s in points:
        for point_t in points:
            for point_r in points:
                strain = np.zeros((6, 24))
                for index, corner in enumerate(corner_list()):
                    factor_x = point_s if corner[0] else 1 - point_s
                    factor_y = point_t if corner[1] else 1 - point_t
                    factor_z = point_r if corner[2] else 1 - point_r
                    slope_x = (2 * corner[0] - 1) * factor_y * factor_z
                    slope_y = factor_x * (2 * corner[1] - 1) * factor_z
                    slope_z = factor_x * factor_y * (2 * corner[2] - 1)
                    column = 3 * index
                    strain[0, column] = slope_x
                    strain[1, column + 1] = slope_y
                    strain[2, column + 2] = slope_z
                    strain[3, column] = slope_y
                    strain[3, column + 1] = slope_x
                    strain[4, column + 1] = slope_z
                    strain[4, column + 2] = slope_y
                    strain[5, column] = slope_z
                    strain[5, column + 2] = slope_x
                result += 0.125 * strain.T @ elastic @ strain
    return result


def modal_matrix():
    pair = np.array([[1.0, 1.0], [-1.0, 1.0]])
    change = np.kron(np.kron(np.kron(pair, pair), pair), np.eye(3))
    back = np.linalg.inv(change)
    modal = back.T @ element_matrix() @ back
    rows = []
    for row in range(24):
        rows.append([(col, float(modal[row, col])) for col in range(24) if abs(modal[row, col]) > 1e-9])
    return rows


MODAL = modal_matrix()
DIAG = float(element_matrix()[0, 0])

DEN, PAS, FR, U, LD, PR = 0, 1, 2, 3, 6, 9
FIELDS = 12

MSG = {
    (0, 1): [(DEN, -4, 4), (PAS, -2, 2), (FR, -1, 1), (LD, -1, 1)],
    (0, -1): [(DEN, N, 4), (PAS, N, 2), (FR, N, 2)],
    (1, 1): [(U + c, -2, 2) for c in range(3)] + [(LD + 1, -1, 1), (LD + 2, -1, 1)],
    (1, -1): [(U + c, N, 3) for c in range(3)] + [(LD + c, N, 2) for c in range(3)],
    (2, -1): [(PR + c, N, 1) for c in range(3)],
    (3, 1): [(c, -2, 2) for c in range(3)],
    (3, -1): [(c, N, 2) for c in range(3)],
}
DIAG_ROWS = {
    (0, 1): (4, 4), (0, -1): (0, 4),
    (1, 1): (6, 2), (1, -1): (0, 3),
    (2, -1): (0, 1),
    (3, 1): (6, 2), (3, -1): (0, 2),
}


def units(msg, way):
    return sum(count for _, _, count in MSG[msg, way])


def pad8(count):
    return (count + 7) // 8 * 8


def routes():
    found = []
    for msg in range(4):
        for dx in (-1, 0, 1):
            for dy in (-1, 0, 1):
                if (dx, dy) == (0, 0):
                    continue
                if (dx and (msg, dx) not in MSG) or (dy and (msg, dy) not in MSG):
                    continue
                found.append((msg, dx, dy))
    return found


RELAYED = (0, 1, 2)


def is_relay(route):
    return route[0] in RELAYED and route[1] != 0 and route[2] != 0


ROUTES = sorted(routes(), key=lambda r: (r[0], r[1] != 0, r[1] != 0 and r[2] != 0))
STAGES = [(msg, axis, way) for (msg, way) in MSG for axis in (0, 1)]


def stage_shape(msg, axis, way):
    if axis == 0:
        return (units(msg, way), N, NZ)
    return (N, pad8(units(msg, way)), NZ)


def route_shape(msg, dx, dy):
    if dy == 0:
        return stage_shape(msg, 0, dx)
    if dx == 0:
        return stage_shape(msg, 1, dy)
    return (DIAG_ROWS[msg, dx][1], pad8(units(msg, dy)), NZ)


def zshift(value, amount):
    lane = lax.broadcasted_iota(jnp.int32, value.shape, value.ndim - 1)
    moved = pltpu.roll(value, (-amount) % NZ, value.ndim - 1)
    keep = (lane < NZ - amount) if amount > 0 else (lane >= -amount)
    return jnp.where(keep, moved, 0.0)


def yshift(value, amount):
    return pltpu.roll(value, (-amount) % value.shape[-2], value.ndim - 2)


def filter_row(rows):
    across = [rows[2], rows[1] + rows[3], rows[0] + rows[4]]
    total = None
    for dz in range(3):
        plane = None
        for dy in range(3):
            part = None
            for dx in range(3):
                square = dx * dx + dy * dy + dz * dz
                if square < 9:
                    term = (RMIN - math.sqrt(square)) * across[dx]
                    part = term if part is None else part + term
            if part is None:
                continue
            if dy:
                part = yshift(part, dy) + yshift(part, -dy)
            plane = part if plane is None else plane + part
        if dz:
            plane = zshift(plane, dz) + zshift(plane, -dz)
        total = plane if total is None else total + plane
    return total


def transform(value):
    up = zshift(value, 1)
    out = [value + up, up - value]
    ups = [yshift(v, 1) for v in out]
    return [out[0] + ups[0], out[1] + ups[1], ups[0] - out[0], ups[1] - out[1]]


def put_transform(held, row, values):
    for c in range(3):
        for k, value in enumerate(transform(values[c])):
            held[4 * c + k, row] = value


def modes(held, row, part=slice(None)):
    out = [None] * 24
    for c in range(3):
        for k in range(4):
            low, high = held[4 * c + k, row, part, :], held[4 * c + k, row + 1, part, :]
            out[3 * k + c] = low + high
            out[12 + 3 * k + c] = high - low
    return out


def stress(mode):
    out = []
    for row in MODAL:
        total = None
        for col, weight in row:
            term = weight * mode[col]
            total = term if total is None else total + term
        out.append(total)
    return out


def dot_modes(first, second):
    total = None
    for a, b in zip(first, second):
        if b is not None:
            total = a * b if total is None else total + a * b
    return total


def spread_forces(held, work, stiff, low, high):
    for k in range(12):
        work[k, low] = jnp.zeros((L, NZ), jnp.float32)

    def step(row, carry):
        scale = stiff[row]
        force = stress(modes(held, row))
        for c in range(3):
            for k in range(4):
                even, odd = force[3 * k + c], force[12 + 3 * k + c]
                odd = odd * scale
                slot = 4 * c + k
                if even is None:
                    work[slot, row] = work[slot, row] - odd
                    work[slot, row + 1] = odd
                else:
                    even = even * scale
                    work[slot, row] = work[slot, row] + (even - odd)
                    work[slot, row + 1] = even + odd
        return carry

    lax.fori_loop(low, high, step, 0)


def node_forces(work, row, c):
    out = []
    for z in range(2):
        even, odd = work[4 * c + z, row], work[4 * c + 2 + z, row]
        out.append((even - odd) + yshift(even + odd, -1))
    return (out[0] - out[1]) + zshift(out[0] + out[1], -1)


def kernel(size_x, size_y, *refs):
    inputs, refs = refs[:7], refs[7:]
    (sens, adjoint), refs = refs[:2], refs[2:]
    held, refs = refs[:7], refs[7:]
    density, passive, fixed, load_nodes, port, guess, primal = held
    stages, refs = dict(zip(STAGES, refs)), refs[len(STAGES):]
    lands, refs = dict(zip(ROUTES, refs)), refs[len(ROUTES):]
    (ext, mask, weight, phys, slope, stiff, factor, res_z, q, inv, tu, td, tq, tp, work, sp,
     red1, red2, acc, send_sem, recv_sem, red_send, red_recv, in_sem) = refs
    loads = [pltpu.make_async_copy(a, b, in_sem.at[k]) for k, (a, b) in enumerate(zip(inputs, held))]
    for item in loads:
        item.start()
    gx, gy = lax.axis_index("gx"), lax.axis_index("gy")
    lower = 4
    upper = size_x // lower * size_y
    group, rank = gx // lower, gx % lower
    upper_rank = group * size_y + gy

    def there(dx, dy):
        ok = None
        for pos, size, d in ((gx, size_x, dx), (gy, size_y, dy)):
            if d:
                this = (pos + d >= 0) & (pos + d < size)
                ok = this if ok is None else ok & this
        return ok

    def peer1(k):
        return (group * lower + (rank + k) % lower, gy)

    def peer2(k):
        other = (upper_rank + k) % upper
        return ((other // size_y) * lower + rank, other % size_y)

    barrier = pltpu.get_barrier_semaphore()
    expected = jnp.int32(lower - 1 + upper - 1)
    for dx in (-1, 0, 1):
        for dy in (-1, 0, 1):
            if (dx, dy) != (0, 0):
                ok = there(dx, dy)
                expected = expected + ok.astype(jnp.int32)

                @pl.when(ok)
                def _():
                    pl.semaphore_signal(barrier, inc=1, device_id=(gx + dx, gy + dy), device_id_type=MESH)
    for k in range(1, lower):
        pl.semaphore_signal(barrier, inc=1, device_id=peer1(k), device_id_type=MESH)
    for k in range(1, upper):
        pl.semaphore_signal(barrier, inc=1, device_id=peer2(k), device_id_type=MESH)

    sub = lax.broadcasted_iota(jnp.int32, (L, NZ), 0)
    at_y = gy * N - W + sub
    inside_y = ((at_y >= 0) & (at_y < size_y * N)).astype(jnp.float32)
    owned = ((sub >= W) & (sub < W + N)).astype(jnp.float32)

    def inside_x(i):
        at_x = gx * N - W + i
        return ((at_x >= 0) & (at_x < size_x * N)).astype(jnp.float32)

    def weigh(i, carry):
        total = filter_row([inside_x(i + d) * inside_y for d in range(-2, 3)])
        weight[i] = 1.0 / jnp.where(total > 0.0, total, 1.0)
        return carry

    lax.fori_loop(2, 14, weigh, 0)

    own = slice(W, W + N)
    def clear(i, carry):
        for f in range(FIELDS):
            ext[f, i] = jnp.zeros((L, NZ), jnp.float32)
        for c in range(3):
            sp[c, i] = jnp.zeros((L, NZ), jnp.float32)
        return carry

    lax.fori_loop(0, L, clear, 0)
    for item in loads:
        item.wait()

    def fill(i, carry):
        free = (1 - fixed[i]).astype(jnp.float32)
        solid = passive[i] == 1
        loaded = free * load_nodes[i].astype(jnp.float32)
        ext[DEN, W + i, own, :] = jnp.where(solid, 1.0, density[i])
        ext[PAS, W + i, own, :] = passive[i].astype(jnp.float32)
        ext[FR, W + i, own, :] = free
        for c in range(3):
            ext[U + c, W + i, own, :] = free * guess[c, i]
            ext[LD + c, W + i, own, :] = loaded * port[c, i]
            ext[PR + c, W + i, own, :] = free * primal[c, i]
        return carry

    lax.fori_loop(0, N, fill, 0)

    def pack(msg, source):
        for way in (1, -1):
            if (msg, way) not in MSG:
                continue
            flat_x, flat_y = stages[msg, 0, way], stages[msg, 1, way]
            at = 0
            for f, first, count in MSG[msg, way]:
                start = W + (first + N if way == 1 else first - N)
                flat_x[at:at + count] = source[f, start:start + count, own, :]
                flat_y[:, at:at + count, :] = source[f, own, start:start + count, :]
                at += count
            if at < flat_y.shape[1]:
                flat_y[:, at:, :] = jnp.zeros((N, flat_y.shape[1] - at, NZ), jnp.float32)

    def copy(route):
        msg, dx, dy = route
        at = ROUTES.index(route)
        if dy == 0:
            source = stages[msg, 0, dx]
        elif dx == 0:
            source = stages[msg, 1, dy]
        else:
            first, count = DIAG_ROWS[msg, dx]
            if msg in RELAYED:
                source = lands[msg, 0, dy].at[first:first + count]
            else:
                source = stages[msg, 1, dy].at[first:first + count]
        return pltpu.make_async_remote_copy(
            src_ref=source,
            dst_ref=lands[route],
            send_sem=send_sem.at[at],
            recv_sem=recv_sem.at[at],
            device_id=(gx + dx, gy if dx and msg in RELAYED else gy + dy),
            device_id_type=MESH,
        )

    def send(msg):
        for route in ROUTES:
            if route[0] == msg and not is_relay(route):
                @pl.when(there(route[1], route[2]))
                def _():
                    copy(route).start()

    def receive(msg, target):
        for route in ROUTES:
            if route[0] != msg:
                continue
            _, dx, dy = route

            @pl.when(there(-dx, -dy))
            def _():
                copy(route).wait_recv()
                land = lands[route]
                if dx == 0:
                    for other in ROUTES:
                        if other[0] == msg and other[2] == dy and is_relay(other):
                            @pl.when(there(other[1], 0))
                            def _():
                                copy(other).start()
                at = 0
                for f, first, count in MSG[msg, dy if dy else dx]:
                    begin = W + first
                    if dy == 0:
                        target[f, begin:begin + count, own, :] = land[at:at + count]
                    elif dx == 0:
                        target[f, own, begin:begin + count, :] = land[:, at:at + count, :]
                    else:
                        source, rows = DIAG_ROWS[msg, dx]
                        row = W + (source - N if dx == 1 else source + N)
                        target[f, row:row + rows, begin:begin + count, :] = land[:, at:at + count, :]
                    at += count

    def finish(msg):
        for route in ROUTES:
            if route[0] == msg:
                _, dx, dy = route

                @pl.when(there(dx, 0) & there(0, -dy) if is_relay(route) else there(dx, dy))
                def _():
                    copy(route).wait_send()

    pack(0, ext)
    pl.semaphore_wait(barrier, expected)
    send(0)
    pack(1, ext)
    send(1)
    pack(2, ext)
    send(2)

    receive(0, ext)
    denom = 2.0 * math.tanh(BETA * ETA)

    def densities(i, carry):
        filtered = filter_row([ext[DEN, i + d] for d in range(-2, 3)]) * weight[i]
        bent = jnp.tanh(BETA * (filtered - ETA))
        solid = ext[PAS, i]
        physical = jnp.where(solid == 1.0, 1.0, (math.tanh(BETA * ETA) + bent) / denom)
        square = physical * physical
        stiff[i] = (EMIN + (1.0 - EMIN) * (square * physical)) * (inside_x(i) * inside_y)
        gain = BETA * (1.0 - bent * bent) / denom
        factor[i] = (-3.0 * (1.0 - EMIN)) * square * gain * (1.0 - solid) * weight[i]
        return carry

    lax.fori_loop(2, 14, densities, 0)

    receive(1, ext)

    def load_u(i, carry):
        put_transform(tu, i, [ext[U + c, i] for c in range(3)])
        return carry

    lax.fori_loop(2, 15, load_u, 0)
    spread_forces(tu, work, stiff, 2, 14)
    acc[...] = jnp.zeros_like(acc)

    def is_owned(i):
        return ((i >= W) & (i < W + N)).astype(jnp.float32) * owned

    def residuals(i, carry):
        free = ext[FR, i]
        pair = stiff[i] + stiff[i - 1]
        pair = pair + yshift(pair, -1)
        total = DIAG * (pair + zshift(pair, -1))
        inverse = free / jnp.where(total > 0.0, total, 1.0)
        inv[i] = inverse
        dot = None
        values = []
        for c in range(3):
            residual = ext[LD + c, i] - free * node_forces(work, i, c)
            value = inverse * residual
            res_z[c, i] = value
            values.append(value)
            dot = residual * value if dot is None else dot + residual * value
        put_transform(td, i, values)
        acc[0] = acc[0] + is_owned(i) * dot
        return carry

    lax.fori_loop(3, 14, residuals, 0)
    spread_forces(td, work, stiff, 3, 13)

    def images(i, carry):
        free, inverse = ext[FR, i], inv[i]
        dot_w = dot_q = None
        values = []
        for c in range(3):
            image = free * node_forces(work, i, c)
            value = inverse * image
            q[c, i] = value
            values.append(value)
            first, second = image * res_z[c, i], image * value
            dot_w = first if dot_w is None else dot_w + first
            dot_q = second if dot_q is None else dot_q + second
        put_transform(tq, i, values)
        acc[1] = acc[1] + is_owned(i) * dot_w
        acc[2] = acc[2] + is_owned(i) * dot_q
        return carry

    lax.fori_loop(4, 13, images, 0)

    def curvature(i, total):
        mode = modes(tq, i, own)
        return total + stiff[i, own, :] * dot_modes(mode, stress(mode))

    last = lax.fori_loop(W, W + N, curvature, jnp.zeros((N, NZ), jnp.float32))

    parts = []
    for value in (acc[0], acc[1], acc[2], last):
        line = jnp.sum(value, axis=0, keepdims=True)
        parts.append(line[:, :128] + line[:, 128:])
    for k, part in enumerate(parts):
        red1[0, k:k + 1, :] = part
    red1[0, 4:8, :] = jnp.zeros((4, 128), jnp.float32)

    def reduce_copy(buf, k, base, target):
        return pltpu.make_async_remote_copy(
            src_ref=buf.at[0],
            dst_ref=buf.at[k],
            send_sem=red_send.at[base + k],
            recv_sem=red_recv.at[base + k],
            device_id=target,
            device_id_type=MESH,
        )

    first_copies = [reduce_copy(red1, k, 0, peer1(k)) for k in range(1, lower)]
    for item in first_copies:
        item.start()

    receive(2, ext)

    def load_p(i, carry):
        put_transform(tp, i, [ext[PR + c, i] for c in range(3)])
        return carry

    lax.fori_loop(4, 13, load_p, 0)

    for item in first_copies:
        item.wait_recv()
    total = red1[0]
    for k in range(1, lower):
        total = total + red1[k]
    red2[0] = total
    second_copies = [reduce_copy(red2, k, lower, peer2(k)) for k in range(1, upper)]
    for item in second_copies:
        item.start()

    def energies(i, carry):
        force = stress(modes(tp, i, own))
        scale = factor[i, own, :]
        for k, held in enumerate((tu, td, tq)):
            sp[k, i, own, :] = scale * dot_modes(modes(held, i, own), force)
        return carry

    lax.fori_loop(W, W + N, energies, 0)
    pack(3, sp)
    send(3)
    receive(3, sp)

    for item in second_copies:
        item.wait_recv()
    total = red2[0]
    for k in range(1, upper):
        total = total + red2[k]
    rz, dw, wq, qv = [jnp.sum(total[k:k + 1, :], axis=1, keepdims=True) for k in range(4)]
    alpha = rz / dw
    after = alpha * alpha * wq - rz
    grow = 1.0 + after / rz
    curve = grow * grow * dw - 2.0 * alpha * grow * wq + alpha * alpha * qv
    beyond = after / curve
    coef_d = alpha + beyond * grow
    coef_q = -beyond * alpha

    def join(i, carry):
        mask[i] = sp[0, i] + coef_d * sp[1, i] + coef_q * sp[2, i]
        return carry

    lax.fori_loop(2, 14, join, 0)

    def result(i, carry):
        row = W + i
        value = filter_row([mask[row + d] for d in range(-2, 3)])
        mine = (1.0 - ext[PAS, row]) * value
        sens[i] = mine[own]
        for c in range(3):
            adjoint[c, i] = (ext[U + c, row, own, :] + coef_d * res_z[c, row, own, :]
                             + coef_q * q[c, row, own, :])
        return carry

    lax.fori_loop(0, N, result, 0)
    for msg in range(4):
        finish(msg)
    for item in first_copies + second_copies:
        item.wait_send()


def local(size_x, size_y, *arrays):
    f32 = jnp.float32
    upper = size_x // 4 * size_y
    scratch = [pltpu.VMEM(array.shape, array.dtype) for array in arrays]
    scratch += [pltpu.VMEM(stage_shape(*stage), f32) for stage in STAGES]
    scratch += [pltpu.VMEM(route_shape(*route), f32) for route in ROUTES]
    plain = pltpu.VMEM((L, L, NZ), f32)
    three = pltpu.VMEM((3, L, L, NZ), f32)
    twelve = pltpu.VMEM((12, L, L, NZ), f32)
    scratch += [twelve, plain, plain, plain, plain, plain, plain, three, three, plain]
    scratch += [twelve] * 5 + [three]
    scratch += [
        pltpu.VMEM((4, 8, 128), f32),
        pltpu.VMEM((upper, 8, 128), f32),
        pltpu.VMEM((3, L, NZ), f32),
        pltpu.SemaphoreType.DMA((len(ROUTES),)),
        pltpu.SemaphoreType.DMA((len(ROUTES),)),
        pltpu.SemaphoreType.DMA((4 + upper,)),
        pltpu.SemaphoreType.DMA((4 + upper,)),
        pltpu.SemaphoreType.DMA((7,)),
    ]
    vmem = pl.BlockSpec(memory_space=pltpu.VMEM)
    return pl.pallas_call(
        lambda *refs: kernel(size_x, size_y, *refs),
        out_shape=(
            jax.ShapeDtypeStruct((N, N, NZ), f32),
            jax.ShapeDtypeStruct((3, N, N, NZ), f32),
        ),
        in_specs=[pl.BlockSpec(memory_space=pltpu.HBM)] * 7,
        out_specs=(vmem, vmem),
        scratch_shapes=scratch,
        compiler_params=pltpu.CompilerParams(
            collective_id=0, has_side_effects=True, vmem_limit_bytes=65000 * 1024
        ),
    )(*arrays)


def solution(mesh):
    grid = P("gx", "gy", None)
    field = P(None, "gx", "gy", None)
    size_x, size_y = mesh.shape["gx"], mesh.shape["gy"]
    return jax.shard_map(
        lambda *arrays: local(size_x, size_y, *arrays),
        mesh=mesh,
        in_specs=(grid, grid, grid, grid, field, field, field),
        out_specs=(grid, field),
        check_vma=False,
    )
```

```python
import math

import jax
import jax.numpy as jnp
import numpy as np
from jax import lax
from jax.experimental import pallas as pl
from jax.experimental.pallas import tpu as pltpu
from jax.sharding import PartitionSpec as P

EMIN = 0.01
BETA = 4.0
ETA = 0.5
RMIN = 3.0
N = 8
W = 4
L = N + 2 * W
NZ = 256
MESH = pl.DeviceIdType.MESH


def corner_list():
    return [
        (along_x, along_y, along_z)
        for along_x in (0, 1)
        for along_y in (0, 1)
        for along_z in (0, 1)
    ]


def element_matrix():
    poisson = 0.3
    lame = poisson / ((1 + poisson) * (1 - 2 * poisson))
    shear = 0.5 / (1 + poisson)
    elastic = np.zeros((6, 6))
    elastic[:3, :3] = lame
    for index in range(3):
        elastic[index, index] += 2 * shear
        elastic[index + 3, index + 3] = shear
    points = [0.5 - 0.5 / math.sqrt(3.0), 0.5 + 0.5 / math.sqrt(3.0)]
    result = np.zeros((24, 24))
    for point_s in points:
        for point_t in points:
            for point_r in points:
                strain = np.zeros((6, 24))
                for index, corner in enumerate(corner_list()):
                    factor_x = point_s if corner[0] else 1 - point_s
                    factor_y = point_t if corner[1] else 1 - point_t
                    factor_z = point_r if corner[2] else 1 - point_r
                    slope_x = (2 * corner[0] - 1) * factor_y * factor_z
                    slope_y = factor_x * (2 * corner[1] - 1) * factor_z
                    slope_z = factor_x * factor_y * (2 * corner[2] - 1)
                    column = 3 * index
                    strain[0, column] = slope_x
                    strain[1, column + 1] = slope_y
                    strain[2, column + 2] = slope_z
                    strain[3, column] = slope_y
                    strain[3, column + 1] = slope_x
                    strain[4, column + 1] = slope_z
                    strain[4, column + 2] = slope_y
                    strain[5, column] = slope_z
                    strain[5, column + 2] = slope_x
                result += 0.125 * strain.T @ elastic @ strain
    return result


def modal_matrix():
    pair = np.array([[1.0, 1.0], [-1.0, 1.0]])
    change = np.kron(np.kron(np.kron(pair, pair), pair), np.eye(3))
    back = np.linalg.inv(change)
    modal = back.T @ element_matrix() @ back
    rows = []
    for row in range(24):
        rows.append([(col, float(modal[row, col])) for col in range(24) if abs(modal[row, col]) > 1e-9])
    return rows


MODAL = modal_matrix()
DIAG = float(element_matrix()[0, 0])

DEN, PAS, FR, U, LD, PR = 0, 1, 2, 3, 6, 9
FIELDS = 12

MSG = {
    (0, 1): [(DEN, -4, 4), (PAS, -2, 2), (FR, -1, 1), (LD, -1, 1)],
    (0, -1): [(DEN, N, 4), (PAS, N, 2), (FR, N, 2)],
    (1, 1): [(U + c, -2, 2) for c in range(3)] + [(LD + 1, -1, 1), (LD + 2, -1, 1)],
    (1, -1): [(U + c, N, 3) for c in range(3)] + [(LD + c, N, 2) for c in range(3)],
    (2, -1): [(PR + c, N, 1) for c in range(3)],
    (3, 1): [(c, -2, 2) for c in range(3)],
    (3, -1): [(c, N, 2) for c in range(3)],
}
DIAG_ROWS = {
    (0, 1): (4, 4), (0, -1): (0, 4),
    (1, 1): (6, 2), (1, -1): (0, 3),
    (2, -1): (0, 1),
    (3, 1): (6, 2), (3, -1): (0, 2),
}


def units(msg, way):
    return sum(count for _, _, count in MSG[msg, way])


def pad8(count):
    return (count + 7) // 8 * 8


def routes():
    found = []
    for msg in range(4):
        for dx in (-1, 0, 1):
            for dy in (-1, 0, 1):
                if (dx, dy) == (0, 0):
                    continue
                if (dx and (msg, dx) not in MSG) or (dy and (msg, dy) not in MSG):
                    continue
                found.append((msg, dx, dy))
    return found


ROUTES = routes()
STAGES = [(msg, axis, way) for (msg, way) in MSG for axis in (0, 1)]


def stage_shape(msg, axis, way):
    if axis == 0:
        return (units(msg, way), N, NZ)
    return (N, pad8(units(msg, way)), NZ)


def route_shape(msg, dx, dy):
    if dy == 0:
        return stage_shape(msg, 0, dx)
    if dx == 0:
        return stage_shape(msg, 1, dy)
    return (DIAG_ROWS[msg, dx][1], pad8(units(msg, dy)), NZ)


def zshift(value, amount):
    lane = lax.broadcasted_iota(jnp.int32, value.shape, value.ndim - 1)
    moved = pltpu.roll(value, (-amount) % NZ, value.ndim - 1)
    keep = (lane < NZ - amount) if amount > 0 else (lane >= -amount)
    return jnp.where(keep, moved, 0.0)


def yshift(value, amount):
    return pltpu.roll(value, (-amount) % value.shape[-2], value.ndim - 2)


def filter_row(rows):
    across = [rows[2], rows[1] + rows[3], rows[0] + rows[4]]
    total = None
    for dz in range(3):
        plane = None
        for dy in range(3):
            part = None
            for dx in range(3):
                square = dx * dx + dy * dy + dz * dz
                if square < 9:
                    term = (RMIN - math.sqrt(square)) * across[dx]
                    part = term if part is None else part + term
            if part is None:
                continue
            if dy:
                part = yshift(part, dy) + yshift(part, -dy)
            plane = part if plane is None else plane + part
        if dz:
            plane = zshift(plane, dz) + zshift(plane, -dz)
        total = plane if total is None else total + plane
    return total


def transform(value):
    up = zshift(value, 1)
    out = [value + up, up - value]
    ups = [yshift(v, 1) for v in out]
    return [out[0] + ups[0], out[1] + ups[1], ups[0] - out[0], ups[1] - out[1]]


def put_transform(held, row, values):
    for c in range(3):
        for k, value in enumerate(transform(values[c])):
            held[4 * c + k, row] = value


def modes(held, row, part=slice(None)):
    out = [None] * 24
    for c in range(3):
        for k in range(4):
            low, high = held[4 * c + k, row, part, :], held[4 * c + k, row + 1, part, :]
            out[3 * k + c] = low + high
            out[12 + 3 * k + c] = high - low
    return out


def stress(mode):
    out = []
    for row in MODAL:
        total = None
        for col, weight in row:
            term = weight * mode[col]
            total = term if total is None else total + term
        out.append(total)
    return out


def dot_modes(first, second):
    total = None
    for a, b in zip(first, second):
        if b is not None:
            total = a * b if total is None else total + a * b
    return total


def spread_forces(held, work, stiff, low, high):
    for k in range(12):
        work[k, low] = jnp.zeros((L, NZ), jnp.float32)

    def step(row, carry):
        scale = stiff[row]
        force = stress(modes(held, row))
        for c in range(3):
            for k in range(4):
                even, odd = force[3 * k + c], force[12 + 3 * k + c]
                odd = odd * scale
                slot = 4 * c + k
                if even is None:
                    work[slot, row] = work[slot, row] - odd
                    work[slot, row + 1] = odd
                else:
                    even = even * scale
                    work[slot, row] = work[slot, row] + (even - odd)
                    work[slot, row + 1] = even + odd
        return carry

    lax.fori_loop(low, high, step, 0)


def node_forces(work, row, c):
    out = []
    for z in range(2):
        even, odd = work[4 * c + z, row], work[4 * c + 2 + z, row]
        out.append((even - odd) + yshift(even + odd, -1))
    return (out[0] - out[1]) + zshift(out[0] + out[1], -1)


def kernel(size_x, size_y, *refs):
    inputs, refs = refs[:7], refs[7:]
    (sens, adjoint), refs = refs[:2], refs[2:]
    held, refs = refs[:7], refs[7:]
    density, passive, fixed, load_nodes, port, guess, primal = held
    stages, refs = dict(zip(STAGES, refs)), refs[len(STAGES):]
    lands, refs = dict(zip(ROUTES, refs)), refs[len(ROUTES):]
    (ext, mask, weight, phys, slope, stiff, factor, res_z, q, inv, tu, td, tq, tp, work, sp,
     red1, red2, acc, send_sem, recv_sem, red_send, red_recv, in_sem) = refs
    loads = [pltpu.make_async_copy(a, b, in_sem.at[k]) for k, (a, b) in enumerate(zip(inputs, held))]
    for item in loads:
        item.start()
    gx, gy = lax.axis_index("gx"), lax.axis_index("gy")
    lower = 4
    upper = size_x // lower * size_y
    group, rank = gx // lower, gx % lower
    upper_rank = group * size_y + gy

    def there(dx, dy):
        ok = None
        for pos, size, d in ((gx, size_x, dx), (gy, size_y, dy)):
            if d:
                this = (pos + d >= 0) & (pos + d < size)
                ok = this if ok is None else ok & this
        return ok

    def peer1(k):
        return (group * lower + (rank + k) % lower, gy)

    def peer2(k):
        other = (upper_rank + k) % upper
        return ((other // size_y) * lower + rank, other % size_y)

    barrier = pltpu.get_barrier_semaphore()
    expected = jnp.int32(lower - 1 + upper - 1)
    for dx in (-1, 0, 1):
        for dy in (-1, 0, 1):
            if (dx, dy) != (0, 0):
                ok = there(dx, dy)
                expected = expected + ok.astype(jnp.int32)

                @pl.when(ok)
                def _():
                    pl.semaphore_signal(barrier, inc=1, device_id=(gx + dx, gy + dy), device_id_type=MESH)
    for k in range(1, lower):
        pl.semaphore_signal(barrier, inc=1, device_id=peer1(k), device_id_type=MESH)
    for k in range(1, upper):
        pl.semaphore_signal(barrier, inc=1, device_id=peer2(k), device_id_type=MESH)

    sub = lax.broadcasted_iota(jnp.int32, (L, NZ), 0)
    at_y = gy * N - W + sub
    inside_y = ((at_y >= 0) & (at_y < size_y * N)).astype(jnp.float32)
    owned = ((sub >= W) & (sub < W + N)).astype(jnp.float32)

    def inside_x(i):
        at_x = gx * N - W + i
        return ((at_x >= 0) & (at_x < size_x * N)).astype(jnp.float32)

    def weigh(i, carry):
        total = filter_row([inside_x(i + d) * inside_y for d in range(-2, 3)])
        weight[i] = 1.0 / jnp.where(total > 0.0, total, 1.0)
        return carry

    lax.fori_loop(2, 14, weigh, 0)

    own = slice(W, W + N)
    def clear(i, carry):
        for f in range(FIELDS):
            ext[f, i] = jnp.zeros((L, NZ), jnp.float32)
        for c in range(3):
            sp[c, i] = jnp.zeros((L, NZ), jnp.float32)
        return carry

    lax.fori_loop(0, L, clear, 0)
    for item in loads:
        item.wait()

    def fill(i, carry):
        free = (1 - fixed[i]).astype(jnp.float32)
        solid = passive[i] == 1
        loaded = free * load_nodes[i].astype(jnp.float32)
        ext[DEN, W + i, own, :] = jnp.where(solid, 1.0, density[i])
        ext[PAS, W + i, own, :] = passive[i].astype(jnp.float32)
        ext[FR, W + i, own, :] = free
        for c in range(3):
            ext[U + c, W + i, own, :] = free * guess[c, i]
            ext[LD + c, W + i, own, :] = loaded * port[c, i]
            ext[PR + c, W + i, own, :] = free * primal[c, i]
        return carry

    lax.fori_loop(0, N, fill, 0)

    def pack(msg, source):
        for way in (1, -1):
            if (msg, way) not in MSG:
                continue
            flat_x, flat_y = stages[msg, 0, way], stages[msg, 1, way]
            at = 0
            for f, first, count in MSG[msg, way]:
                start = W + (first + N if way == 1 else first - N)
                flat_x[at:at + count] = source[f, start:start + count, own, :]
                flat_y[:, at:at + count, :] = source[f, own, start:start + count, :]
                at += count
            if at < flat_y.shape[1]:
                flat_y[:, at:, :] = jnp.zeros((N, flat_y.shape[1] - at, NZ), jnp.float32)

    def copy(route):
        msg, dx, dy = route
        at = ROUTES.index(route)
        if dy == 0:
            source = stages[msg, 0, dx]
        elif dx == 0:
            source = stages[msg, 1, dy]
        else:
            first, count = DIAG_ROWS[msg, dx]
            source = stages[msg, 1, dy].at[first:first + count]
        return pltpu.make_async_remote_copy(
            src_ref=source,
            dst_ref=lands[route],
            send_sem=send_sem.at[at],
            recv_sem=recv_sem.at[at],
            device_id=(gx + dx, gy + dy),
            device_id_type=MESH,
        )

    def send(msg):
        for route in ROUTES:
            if route[0] == msg:
                @pl.when(there(route[1], route[2]))
                def _():
                    copy(route).start()

    def receive(msg, target):
        for route in ROUTES:
            if route[0] != msg:
                continue
            _, dx, dy = route

            @pl.when(there(-dx, -dy))
            def _():
                copy(route).wait_recv()
                land = lands[route]
                at = 0
                for f, first, count in MSG[msg, dy if dy else dx]:
                    begin = W + first
                    if dy == 0:
                        target[f, begin:begin + count, own, :] = land[at:at + count]
                    elif dx == 0:
                        target[f, own, begin:begin + count, :] = land[:, at:at + count, :]
                    else:
                        source, rows = DIAG_ROWS[msg, dx]
                        row = W + (source - N if dx == 1 else source + N)
                        target[f, row:row + rows, begin:begin + count, :] = land[:, at:at + count, :]
                    at += count

    def finish(msg):
        for route in ROUTES:
            if route[0] == msg:
                @pl.when(there(route[1], route[2]))
                def _():
                    copy(route).wait_send()

    pack(0, ext)
    pl.semaphore_wait(barrier, expected)
    send(0)
    pack(1, ext)
    send(1)
    pack(2, ext)
    send(2)

    receive(0, ext)
    denom = 2.0 * math.tanh(BETA * ETA)

    def densities(i, carry):
        filtered = filter_row([ext[DEN, i + d] for d in range(-2, 3)]) * weight[i]
        bent = jnp.tanh(BETA * (filtered - ETA))
        solid = ext[PAS, i]
        physical = jnp.where(solid == 1.0, 1.0, (math.tanh(BETA * ETA) + bent) / denom)
        square = physical * physical
        stiff[i] = (EMIN + (1.0 - EMIN) * (square * physical)) * (inside_x(i) * inside_y)
        gain = BETA * (1.0 - bent * bent) / denom
        factor[i] = (-3.0 * (1.0 - EMIN)) * square * gain * (1.0 - solid) * weight[i]
        return carry

    lax.fori_loop(2, 14, densities, 0)

    receive(1, ext)

    def load_u(i, carry):
        put_transform(tu, i, [ext[U + c, i] for c in range(3)])
        return carry

    lax.fori_loop(2, 15, load_u, 0)
    spread_forces(tu, work, stiff, 2, 14)
    acc[...] = jnp.zeros_like(acc)

    def is_owned(i):
        return ((i >= W) & (i < W + N)).astype(jnp.float32) * owned

    def residuals(i, carry):
        free = ext[FR, i]
        pair = stiff[i] + stiff[i - 1]
        pair = pair + yshift(pair, -1)
        total = DIAG * (pair + zshift(pair, -1))
        inverse = free / jnp.where(total > 0.0, total, 1.0)
        inv[i] = inverse
        dot = None
        values = []
        for c in range(3):
            residual = ext[LD + c, i] - free * node_forces(work, i, c)
            value = inverse * residual
            res_z[c, i] = value
            values.append(value)
            dot = residual * value if dot is None else dot + residual * value
        put_transform(td, i, values)
        acc[0] = acc[0] + is_owned(i) * dot
        return carry

    lax.fori_loop(3, 14, residuals, 0)
    spread_forces(td, work, stiff, 3, 13)

    def images(i, carry):
        free, inverse = ext[FR, i], inv[i]
        dot_w = dot_q = None
        values = []
        for c in range(3):
            image = free * node_forces(work, i, c)
            value = inverse * image
            q[c, i] = value
            values.append(value)
            first, second = image * res_z[c, i], image * value
            dot_w = first if dot_w is None else dot_w + first
            dot_q = second if dot_q is None else dot_q + second
        put_transform(tq, i, values)
        acc[1] = acc[1] + is_owned(i) * dot_w
        acc[2] = acc[2] + is_owned(i) * dot_q
        return carry

    lax.fori_loop(4, 13, images, 0)

    def curvature(i, total):
        mode = modes(tq, i, own)
        return total + stiff[i, own, :] * dot_modes(mode, stress(mode))

    last = lax.fori_loop(W, W + N, curvature, jnp.zeros((N, NZ), jnp.float32))

    parts = []
    for value in (acc[0], acc[1], acc[2], last):
        line = jnp.sum(value, axis=0, keepdims=True)
        parts.append(line[:, :128] + line[:, 128:])
    for k, part in enumerate(parts):
        red1[0, k:k + 1, :] = part
    red1[0, 4:8, :] = jnp.zeros((4, 128), jnp.float32)

    def reduce_copy(buf, k, base, target):
        return pltpu.make_async_remote_copy(
            src_ref=buf.at[0],
            dst_ref=buf.at[k],
            send_sem=red_send.at[base + k],
            recv_sem=red_recv.at[base + k],
            device_id=target,
            device_id_type=MESH,
        )

    first_copies = [reduce_copy(red1, k, 0, peer1(k)) for k in range(1, lower)]
    for item in first_copies:
        item.start()

    receive(2, ext)

    def load_p(i, carry):
        put_transform(tp, i, [ext[PR + c, i] for c in range(3)])
        return carry

    lax.fori_loop(4, 13, load_p, 0)

    def energies(i, carry):
        force = stress(modes(tp, i, own))
        scale = factor[i, own, :]
        for k, held in enumerate((tu, td, tq)):
            sp[k, i, own, :] = scale * dot_modes(modes(held, i, own), force)
        return carry

    lax.fori_loop(W, W + N, energies, 0)
    pack(3, sp)
    send(3)

    for item in first_copies:
        item.wait_recv()
    total = red1[0]
    for k in range(1, lower):
        total = total + red1[k]
    red2[0] = total
    second_copies = [reduce_copy(red2, k, lower, peer2(k)) for k in range(1, upper)]
    for item in second_copies:
        item.start()

    receive(3, sp)

    for item in second_copies:
        item.wait_recv()
    total = red2[0]
    for k in range(1, upper):
        total = total + red2[k]
    rz, dw, wq, qv = [jnp.sum(total[k:k + 1, :], axis=1, keepdims=True) for k in range(4)]
    alpha = rz / dw
    after = alpha * alpha * wq - rz
    grow = 1.0 + after / rz
    curve = grow * grow * dw - 2.0 * alpha * grow * wq + alpha * alpha * qv
    beyond = after / curve
    coef_d = alpha + beyond * grow
    coef_q = -beyond * alpha

    def join(i, carry):
        mask[i] = sp[0, i] + coef_d * sp[1, i] + coef_q * sp[2, i]
        return carry

    lax.fori_loop(2, 14, join, 0)

    def result(i, carry):
        row = W + i
        value = filter_row([mask[row + d] for d in range(-2, 3)])
        mine = (1.0 - ext[PAS, row]) * value
        sens[i] = mine[own]
        for c in range(3):
            adjoint[c, i] = (ext[U + c, row, own, :] + coef_d * res_z[c, row, own, :]
                             + coef_q * q[c, row, own, :])
        return carry

    lax.fori_loop(0, N, result, 0)
    for msg in range(4):
        finish(msg)
    for item in first_copies + second_copies:
        item.wait_send()


def local(size_x, size_y, *arrays):
    f32 = jnp.float32
    upper = size_x // 4 * size_y
    scratch = [pltpu.VMEM(array.shape, array.dtype) for array in arrays]
    scratch += [pltpu.VMEM(stage_shape(*stage), f32) for stage in STAGES]
    scratch += [pltpu.VMEM(route_shape(*route), f32) for route in ROUTES]
    plain = pltpu.VMEM((L, L, NZ), f32)
    three = pltpu.VMEM((3, L, L, NZ), f32)
    twelve = pltpu.VMEM((12, L, L, NZ), f32)
    scratch += [twelve, plain, plain, plain, plain, plain, plain, three, three, plain]
    scratch += [twelve] * 5 + [three]
    scratch += [
        pltpu.VMEM((4, 8, 128), f32),
        pltpu.VMEM((upper, 8, 128), f32),
        pltpu.VMEM((3, L, NZ), f32),
        pltpu.SemaphoreType.DMA((len(ROUTES),)),
        pltpu.SemaphoreType.DMA((len(ROUTES),)),
        pltpu.SemaphoreType.DMA((4 + upper,)),
        pltpu.SemaphoreType.DMA((4 + upper,)),
        pltpu.SemaphoreType.DMA((7,)),
    ]
    vmem = pl.BlockSpec(memory_space=pltpu.VMEM)
    return pl.pallas_call(
        lambda *refs: kernel(size_x, size_y, *refs),
        out_shape=(
            jax.ShapeDtypeStruct((N, N, NZ), f32),
            jax.ShapeDtypeStruct((3, N, N, NZ), f32),
        ),
        in_specs=[pl.BlockSpec(memory_space=pltpu.HBM)] * 7,
        out_specs=(vmem, vmem),
        scratch_shapes=scratch,
        compiler_params=pltpu.CompilerParams(
            collective_id=0, has_side_effects=True, vmem_limit_bytes=65000 * 1024
        ),
    )(*arrays)


def solution(mesh):
    grid = P("gx", "gy", None)
    field = P(None, "gx", "gy", None)
    size_x, size_y = mesh.shape["gx"], mesh.shape["gy"]
    return jax.shard_map(
        lambda *arrays: local(size_x, size_y, *arrays),
        mesh=mesh,
        in_specs=(grid, grid, grid, grid, field, field, field),
        out_specs=(grid, field),
        check_vma=False,
    )
```

```python
import math

import jax
import jax.numpy as jnp
import numpy as np
from jax import lax
from jax.experimental import pallas as pl
from jax.experimental.pallas import tpu as pltpu
from jax.sharding import PartitionSpec as P

EMIN = 0.01
BETA = 4.0
ETA = 0.5
RMIN = 3.0
N = 8
W = 4
L = N + 2 * W
NZ = 256
MESH = pl.DeviceIdType.MESH


def corner_list():
    return [
        (along_x, along_y, along_z)
        for along_x in (0, 1)
        for along_y in (0, 1)
        for along_z in (0, 1)
    ]


def element_matrix():
    poisson = 0.3
    lame = poisson / ((1 + poisson) * (1 - 2 * poisson))
    shear = 0.5 / (1 + poisson)
    elastic = np.zeros((6, 6))
    elastic[:3, :3] = lame
    for index in range(3):
        elastic[index, index] += 2 * shear
        elastic[index + 3, index + 3] = shear
    points = [0.5 - 0.5 / math.sqrt(3.0), 0.5 + 0.5 / math.sqrt(3.0)]
    result = np.zeros((24, 24))
    for point_s in points:
        for point_t in points:
            for point_r in points:
                strain = np.zeros((6, 24))
                for index, corner in enumerate(corner_list()):
                    factor_x = point_s if corner[0] else 1 - point_s
                    factor_y = point_t if corner[1] else 1 - point_t
                    factor_z = point_r if corner[2] else 1 - point_r
                    slope_x = (2 * corner[0] - 1) * factor_y * factor_z
                    slope_y = factor_x * (2 * corner[1] - 1) * factor_z
                    slope_z = factor_x * factor_y * (2 * corner[2] - 1)
                    column = 3 * index
                    strain[0, column] = slope_x
                    strain[1, column + 1] = slope_y
                    strain[2, column + 2] = slope_z
                    strain[3, column] = slope_y
                    strain[3, column + 1] = slope_x
                    strain[4, column + 1] = slope_z
                    strain[4, column + 2] = slope_y
                    strain[5, column] = slope_z
                    strain[5, column + 2] = slope_x
                result += 0.125 * strain.T @ elastic @ strain
    return result


def modal_matrix():
    pair = np.array([[1.0, 1.0], [-1.0, 1.0]])
    change = np.kron(np.kron(np.kron(pair, pair), pair), np.eye(3))
    back = np.linalg.inv(change)
    modal = back.T @ element_matrix() @ back
    rows = []
    for row in range(24):
        rows.append([(col, float(modal[row, col])) for col in range(24) if abs(modal[row, col]) > 1e-9])
    return rows


MODAL = modal_matrix()
DIAG = float(element_matrix()[0, 0])

DEN, PAS, FR, U, LD, PR = 0, 1, 2, 3, 6, 9
FIELDS = 12

MSG = {
    (0, 1): [(DEN, -4, 4), (PAS, -2, 2), (FR, -1, 1), (LD, -1, 1)],
    (0, -1): [(DEN, N, 4), (PAS, N, 2), (FR, N, 2)],
    (1, 1): [(U + c, -2, 2) for c in range(3)] + [(LD + 1, -1, 1), (LD + 2, -1, 1)],
    (1, -1): [(U + c, N, 3) for c in range(3)] + [(LD + c, N, 2) for c in range(3)],
    (2, -1): [(PR + c, N, 1) for c in range(3)],
    (3, 1): [(c, -2, 2) for c in range(3)],
    (3, -1): [(c, N, 2) for c in range(3)],
}
DIAG_ROWS = {
    (0, 1): (4, 4), (0, -1): (0, 4),
    (1, 1): (6, 2), (1, -1): (0, 3),
    (2, -1): (0, 1),
    (3, 1): (6, 2), (3, -1): (0, 2),
}


def units(msg, way):
    return sum(count for _, _, count in MSG[msg, way])


def pad8(count):
    return (count + 7) // 8 * 8


def routes():
    found = []
    for msg in range(4):
        for dx in (-1, 0, 1):
            for dy in (-1, 0, 1):
                if (dx, dy) == (0, 0):
                    continue
                if (dx and (msg, dx) not in MSG) or (dy and (msg, dy) not in MSG):
                    continue
                found.append((msg, dx, dy))
    return found


ROUTES = routes()
STAGES = [(msg, axis, way) for (msg, way) in MSG for axis in (0, 1)]


def stage_shape(msg, axis, way):
    if axis == 0:
        return (units(msg, way), N, NZ)
    return (N, pad8(units(msg, way)), NZ)


def route_shape(msg, dx, dy):
    if dy == 0:
        return stage_shape(msg, 0, dx)
    if dx == 0:
        return stage_shape(msg, 1, dy)
    return (DIAG_ROWS[msg, dx][1], pad8(units(msg, dy)), NZ)


def zshift(value, amount):
    lane = lax.broadcasted_iota(jnp.int32, value.shape, value.ndim - 1)
    moved = pltpu.roll(value, (-amount) % NZ, value.ndim - 1)
    keep = (lane < NZ - amount) if amount > 0 else (lane >= -amount)
    return jnp.where(keep, moved, 0.0)


def yshift(value, amount):
    return pltpu.roll(value, (-amount) % value.shape[-2], value.ndim - 2)


def filter_row(rows):
    across = [rows[2], rows[1] + rows[3], rows[0] + rows[4]]
    total = None
    for dz in range(3):
        plane = None
        for dy in range(3):
            part = None
            for dx in range(3):
                square = dx * dx + dy * dy + dz * dz
                if square < 9:
                    term = (RMIN - math.sqrt(square)) * across[dx]
                    part = term if part is None else part + term
            if part is None:
                continue
            if dy:
                part = yshift(part, dy) + yshift(part, -dy)
            plane = part if plane is None else plane + part
        if dz:
            plane = zshift(plane, dz) + zshift(plane, -dz)
        total = plane if total is None else total + plane
    return total


def transform(value):
    up = zshift(value, 1)
    out = [value + up, up - value]
    ups = [yshift(v, 1) for v in out]
    return [out[0] + ups[0], out[1] + ups[1], ups[0] - out[0], ups[1] - out[1]]


def put_transform(held, row, values):
    for c in range(3):
        for k, value in enumerate(transform(values[c])):
            held[4 * c + k, row] = value


def modes(held, row, part=slice(None)):
    out = [None] * 24
    for c in range(3):
        for k in range(4):
            low, high = held[4 * c + k, row, part, :], held[4 * c + k, row + 1, part, :]
            out[3 * k + c] = low + high
            out[12 + 3 * k + c] = high - low
    return out


def stress(mode):
    out = []
    for row in MODAL:
        total = None
        for col, weight in row:
            term = weight * mode[col]
            total = term if total is None else total + term
        out.append(total)
    return out


def dot_modes(first, second):
    total = None
    for a, b in zip(first, second):
        if b is not None:
            total = a * b if total is None else total + a * b
    return total


def spread_forces(held, work, stiff, low, high):
    for k in range(12):
        work[k, low] = jnp.zeros((L, NZ), jnp.float32)

    def step(row, carry):
        scale = stiff[row]
        force = stress(modes(held, row))
        for c in range(3):
            for k in range(4):
                even, odd = force[3 * k + c], force[12 + 3 * k + c]
                odd = odd * scale
                slot = 4 * c + k
                if even is None:
                    work[slot, row] = work[slot, row] - odd
                    work[slot, row + 1] = odd
                else:
                    even = even * scale
                    work[slot, row] = work[slot, row] + (even - odd)
                    work[slot, row + 1] = even + odd
        return carry

    lax.fori_loop(low, high, step, 0)


def node_forces(work, row, c):
    out = []
    for z in range(2):
        even, odd = work[4 * c + z, row], work[4 * c + 2 + z, row]
        out.append((even - odd) + yshift(even + odd, -1))
    return (out[0] - out[1]) + zshift(out[0] + out[1], -1)


def kernel(size_x, size_y, *refs):
    inputs, refs = refs[:7], refs[7:]
    (sens, adjoint), refs = refs[:2], refs[2:]
    held, refs = refs[:7], refs[7:]
    density, passive, fixed, load_nodes, port, guess, primal = held
    stages, refs = dict(zip(STAGES, refs)), refs[len(STAGES):]
    lands, refs = dict(zip(ROUTES, refs)), refs[len(ROUTES):]
    (ext, mask, weight, phys, slope, stiff, factor, res_z, q, inv, tu, td, tq, tp, work, sp,
     red1, red2, acc, send_sem, recv_sem, red_send, red_recv, in_sem) = refs
    loads = [pltpu.make_async_copy(a, b, in_sem.at[k]) for k, (a, b) in enumerate(zip(inputs, held))]
    for item in loads:
        item.start()
    gx, gy = lax.axis_index("gx"), lax.axis_index("gy")
    lower = 4
    upper = size_x // lower * size_y
    group, rank = gx // lower, gx % lower
    upper_rank = group * size_y + gy

    def there(dx, dy):
        ok = None
        for pos, size, d in ((gx, size_x, dx), (gy, size_y, dy)):
            if d:
                this = (pos + d >= 0) & (pos + d < size)
                ok = this if ok is None else ok & this
        return ok

    def peer1(k):
        return (group * lower + (rank + k) % lower, gy)

    def peer2(k):
        other = (upper_rank + k) % upper
        return ((other // size_y) * lower + rank, other % size_y)

    barrier = pltpu.get_barrier_semaphore()
    expected = jnp.int32(lower - 1 + upper - 1)
    for dx in (-1, 0, 1):
        for dy in (-1, 0, 1):
            if (dx, dy) != (0, 0):
                ok = there(dx, dy)
                expected = expected + ok.astype(jnp.int32)

                @pl.when(ok)
                def _():
                    pl.semaphore_signal(barrier, inc=1, device_id=(gx + dx, gy + dy), device_id_type=MESH)
    for k in range(1, lower):
        pl.semaphore_signal(barrier, inc=1, device_id=peer1(k), device_id_type=MESH)
    for k in range(1, upper):
        pl.semaphore_signal(barrier, inc=1, device_id=peer2(k), device_id_type=MESH)

    own = slice(W, W + N)
    def clear(i, carry):
        for f in range(FIELDS):
            ext[f, i] = jnp.zeros((L, NZ), jnp.float32)
        for c in range(3):
            sp[c, i] = jnp.zeros((L, NZ), jnp.float32)
        return carry

    lax.fori_loop(0, L, clear, 0)
    for item in loads:
        item.wait()

    def fill(i, carry):
        free = (1 - fixed[i]).astype(jnp.float32)
        solid = passive[i] == 1
        loaded = free * load_nodes[i].astype(jnp.float32)
        ext[DEN, W + i, own, :] = jnp.where(solid, 1.0, density[i])
        ext[PAS, W + i, own, :] = passive[i].astype(jnp.float32)
        ext[FR, W + i, own, :] = free
        for c in range(3):
            ext[U + c, W + i, own, :] = free * guess[c, i]
            ext[LD + c, W + i, own, :] = loaded * port[c, i]
            ext[PR + c, W + i, own, :] = free * primal[c, i]
        return carry

    lax.fori_loop(0, N, fill, 0)

    def pack(msg, source):
        for way in (1, -1):
            if (msg, way) not in MSG:
                continue
            flat_x, flat_y = stages[msg, 0, way], stages[msg, 1, way]
            at = 0
            for f, first, count in MSG[msg, way]:
                start = W + (first + N if way == 1 else first - N)
                flat_x[at:at + count] = source[f, start:start + count, own, :]
                flat_y[:, at:at + count, :] = source[f, own, start:start + count, :]
                at += count
            if at < flat_y.shape[1]:
                flat_y[:, at:, :] = jnp.zeros((N, flat_y.shape[1] - at, NZ), jnp.float32)

    def copy(route):
        msg, dx, dy = route
        at = ROUTES.index(route)
        if dy == 0:
            source = stages[msg, 0, dx]
        elif dx == 0:
            source = stages[msg, 1, dy]
        else:
            first, count = DIAG_ROWS[msg, dx]
            source = stages[msg, 1, dy].at[first:first + count]
        return pltpu.make_async_remote_copy(
            src_ref=source,
            dst_ref=lands[route],
            send_sem=send_sem.at[at],
            recv_sem=recv_sem.at[at],
            device_id=(gx + dx, gy + dy),
            device_id_type=MESH,
        )

    def send(msg):
        for route in ROUTES:
            if route[0] == msg:
                @pl.when(there(route[1], route[2]))
                def _():
                    copy(route).start()

    def receive(msg, target):
        for route in ROUTES:
            if route[0] != msg:
                continue
            _, dx, dy = route

            @pl.when(there(-dx, -dy))
            def _():
                copy(route).wait_recv()
                land = lands[route]
                at = 0
                for f, first, count in MSG[msg, dy if dy else dx]:
                    begin = W + first
                    if dy == 0:
                        target[f, begin:begin + count, own, :] = land[at:at + count]
                    elif dx == 0:
                        target[f, own, begin:begin + count, :] = land[:, at:at + count, :]
                    else:
                        source, rows = DIAG_ROWS[msg, dx]
                        row = W + (source - N if dx == 1 else source + N)
                        target[f, row:row + rows, begin:begin + count, :] = land[:, at:at + count, :]
                    at += count

    def finish(msg):
        for route in ROUTES:
            if route[0] == msg:
                @pl.when(there(route[1], route[2]))
                def _():
                    copy(route).wait_send()

    pack(0, ext)
    pl.semaphore_wait(barrier, expected)
    send(0)
    pack(1, ext)
    send(1)
    pack(2, ext)
    send(2)

    sub = lax.broadcasted_iota(jnp.int32, (L, NZ), 0)
    at_y = gy * N - W + sub
    inside_y = ((at_y >= 0) & (at_y < size_y * N)).astype(jnp.float32)
    owned = ((sub >= W) & (sub < W + N)).astype(jnp.float32)

    def inside_x(i):
        at_x = gx * N - W + i
        return ((at_x >= 0) & (at_x < size_x * N)).astype(jnp.float32)

    def weigh(i, carry):
        total = filter_row([inside_x(i + d) * inside_y for d in range(-2, 3)])
        weight[i] = 1.0 / jnp.where(total > 0.0, total, 1.0)
        return carry

    lax.fori_loop(2, 14, weigh, 0)

    receive(0, ext)
    denom = 2.0 * math.tanh(BETA * ETA)

    def densities(i, carry):
        filtered = filter_row([ext[DEN, i + d] for d in range(-2, 3)]) * weight[i]
        bent = jnp.tanh(BETA * (filtered - ETA))
        solid = ext[PAS, i]
        physical = jnp.where(solid == 1.0, 1.0, (math.tanh(BETA * ETA) + bent) / denom)
        square = physical * physical
        stiff[i] = (EMIN + (1.0 - EMIN) * (square * physical)) * (inside_x(i) * inside_y)
        gain = BETA * (1.0 - bent * bent) / denom
        factor[i] = (-3.0 * (1.0 - EMIN)) * square * gain * (1.0 - solid) * weight[i]
        return carry

    lax.fori_loop(2, 14, densities, 0)

    receive(1, ext)

    def load_u(i, carry):
        put_transform(tu, i, [ext[U + c, i] for c in range(3)])
        return carry

    lax.fori_loop(2, 15, load_u, 0)
    spread_forces(tu, work, stiff, 2, 14)
    acc[...] = jnp.zeros_like(acc)

    def is_owned(i):
        return ((i >= W) & (i < W + N)).astype(jnp.float32) * owned

    def residuals(i, carry):
        free = ext[FR, i]
        pair = stiff[i] + stiff[i - 1]
        pair = pair + yshift(pair, -1)
        total = DIAG * (pair + zshift(pair, -1))
        inverse = free / jnp.where(total > 0.0, total, 1.0)
        inv[i] = inverse
        dot = None
        values = []
        for c in range(3):
            residual = ext[LD + c, i] - free * node_forces(work, i, c)
            value = inverse * residual
            res_z[c, i] = value
            values.append(value)
            dot = residual * value if dot is None else dot + residual * value
        put_transform(td, i, values)
        acc[0] = acc[0] + is_owned(i) * dot
        return carry

    lax.fori_loop(3, 14, residuals, 0)
    spread_forces(td, work, stiff, 3, 13)

    def images(i, carry):
        free, inverse = ext[FR, i], inv[i]
        dot_w = dot_q = None
        values = []
        for c in range(3):
            image = free * node_forces(work, i, c)
            value = inverse * image
            q[c, i] = value
            values.append(value)
            first, second = image * res_z[c, i], image * value
            dot_w = first if dot_w is None else dot_w + first
            dot_q = second if dot_q is None else dot_q + second
        put_transform(tq, i, values)
        acc[1] = acc[1] + is_owned(i) * dot_w
        acc[2] = acc[2] + is_owned(i) * dot_q
        return carry

    lax.fori_loop(4, 13, images, 0)

    def curvature(i, total):
        mode = modes(tq, i, own)
        return total + stiff[i, own, :] * dot_modes(mode, stress(mode))

    last = lax.fori_loop(W, W + N, curvature, jnp.zeros((N, NZ), jnp.float32))

    parts = []
    for value in (acc[0], acc[1], acc[2], last):
        line = jnp.sum(value, axis=0, keepdims=True)
        parts.append(line[:, :128] + line[:, 128:])
    for k, part in enumerate(parts):
        red1[0, k:k + 1, :] = part
    red1[0, 4:8, :] = jnp.zeros((4, 128), jnp.float32)

    def reduce_copy(buf, k, base, target):
        return pltpu.make_async_remote_copy(
            src_ref=buf.at[0],
            dst_ref=buf.at[k],
            send_sem=red_send.at[base + k],
            recv_sem=red_recv.at[base + k],
            device_id=target,
            device_id_type=MESH,
        )

    first_copies = [reduce_copy(red1, k, 0, peer1(k)) for k in range(1, lower)]
    for item in first_copies:
        item.start()

    receive(2, ext)

    def load_p(i, carry):
        put_transform(tp, i, [ext[PR + c, i] for c in range(3)])
        return carry

    lax.fori_loop(4, 13, load_p, 0)

    for item in first_copies:
        item.wait_recv()
    total = red1[0]
    for k in range(1, lower):
        total = total + red1[k]
    red2[0] = total
    second_copies = [reduce_copy(red2, k, lower, peer2(k)) for k in range(1, upper)]
    for item in second_copies:
        item.start()

    def energies(i, carry):
        force = stress(modes(tp, i, own))
        scale = factor[i, own, :]
        for k, held in enumerate((tu, td, tq)):
            sp[k, i, own, :] = scale * dot_modes(modes(held, i, own), force)
        return carry

    lax.fori_loop(W, W + N, energies, 0)
    pack(3, sp)
    send(3)
    receive(3, sp)

    for item in second_copies:
        item.wait_recv()
    total = red2[0]
    for k in range(1, upper):
        total = total + red2[k]
    rz, dw, wq, qv = [jnp.sum(total[k:k + 1, :], axis=1, keepdims=True) for k in range(4)]
    alpha = rz / dw
    after = alpha * alpha * wq - rz
    grow = 1.0 + after / rz
    curve = grow * grow * dw - 2.0 * alpha * grow * wq + alpha * alpha * qv
    beyond = after / curve
    coef_d = alpha + beyond * grow
    coef_q = -beyond * alpha

    def join(i, carry):
        mask[i] = sp[0, i] + coef_d * sp[1, i] + coef_q * sp[2, i]
        return carry

    lax.fori_loop(2, 14, join, 0)

    def result(i, carry):
        row = W + i
        value = filter_row([mask[row + d] for d in range(-2, 3)])
        mine = (1.0 - ext[PAS, row]) * value
        sens[i] = mine[own]
        for c in range(3):
            adjoint[c, i] = (ext[U + c, row, own, :] + coef_d * res_z[c, row, own, :]
                             + coef_q * q[c, row, own, :])
        return carry

    lax.fori_loop(0, N, result, 0)
    for msg in range(4):
        finish(msg)
    for item in first_copies + second_copies:
        item.wait_send()


def local(size_x, size_y, *arrays):
    f32 = jnp.float32
    upper = size_x // 4 * size_y
    scratch = [pltpu.VMEM(array.shape, array.dtype) for array in arrays]
    scratch += [pltpu.VMEM(stage_shape(*stage), f32) for stage in STAGES]
    scratch += [pltpu.VMEM(route_shape(*route), f32) for route in ROUTES]
    plain = pltpu.VMEM((L, L, NZ), f32)
    three = pltpu.VMEM((3, L, L, NZ), f32)
    twelve = pltpu.VMEM((12, L, L, NZ), f32)
    scratch += [twelve, plain, plain, plain, plain, plain, plain, three, three, plain]
    scratch += [twelve] * 5 + [three]
    scratch += [
        pltpu.VMEM((4, 8, 128), f32),
        pltpu.VMEM((upper, 8, 128), f32),
        pltpu.VMEM((3, L, NZ), f32),
        pltpu.SemaphoreType.DMA((len(ROUTES),)),
        pltpu.SemaphoreType.DMA((len(ROUTES),)),
        pltpu.SemaphoreType.DMA((4 + upper,)),
        pltpu.SemaphoreType.DMA((4 + upper,)),
        pltpu.SemaphoreType.DMA((7,)),
    ]
    vmem = pl.BlockSpec(memory_space=pltpu.VMEM)
    return pl.pallas_call(
        lambda *refs: kernel(size_x, size_y, *refs),
        out_shape=(
            jax.ShapeDtypeStruct((N, N, NZ), f32),
            jax.ShapeDtypeStruct((3, N, N, NZ), f32),
        ),
        in_specs=[pl.BlockSpec(memory_space=pltpu.HBM)] * 7,
        out_specs=(vmem, vmem),
        scratch_shapes=scratch,
        compiler_params=pltpu.CompilerParams(
            collective_id=0, has_side_effects=True, vmem_limit_bytes=65000 * 1024
        ),
    )(*arrays)


def solution(mesh):
    grid = P("gx", "gy", None)
    field = P(None, "gx", "gy", None)
    size_x, size_y = mesh.shape["gx"], mesh.shape["gy"]
    return jax.shard_map(
        lambda *arrays: local(size_x, size_y, *arrays),
        mesh=mesh,
        in_specs=(grid, grid, grid, grid, field, field, field),
        out_specs=(grid, field),
        check_vma=False,
    )
```
